256 devices in a mesh: grp: 2 (over core), seq: 128 (over z, x, y).
Axes of the slice: x: 4, y: 4, z: 8, core: 2. Of those that a mesh axis runs over, the one named last changes fastest.
Arguments:
- latent_large: bfloat16 [4096, 5120], P('seq'), may hold values from -6 to 6
- latent_small: bfloat16 [4096, 1536], P('seq'), may hold values from -6 to 6
- gain_large: float32 [5120], replicated, may hold values from 0.1 to 1.9
- gain_small: float32 [1536], replicated, may hold values from 0.1 to 1.9
- qkv_large: bfloat16 [5120, 12288], P(None, ('grp', 'seq')), may hold values from -0.08385255 to 0.08385255
- qkv_small: bfloat16 [1536, 3072], P(None, ('grp', 'seq')), may hold values from -0.15309311 to 0.15309311
- mix_large: bfloat16 [4096, 64], P('grp'), may hold values from -0.09375 to 0.09375
- mix_small: bfloat16 [1024, 64], P('grp'), may hold values from -0.1875 to 0.1875
- head_large: bfloat16 [5120, 64], replicated, may hold values from -0.078125 to 0.078125
- head_small: bfloat16 [1536, 64], replicated, may hold values from -0.15625 to 0.15625
Outputs:
- guided: float32 [4096, 64], P('seq')
The draws below stay inside these ranges and needn't reach their ends.
All inputs are finite; a program needn't handle non-finite values.
Results may differ from the reference program's by a relative error of at most 0.00095.
The reference program's roundings to bfloat16 on the way count: a program that leaves them out, or rounds other values in their place, can miss the bound.
Values may be sent and summed in bfloat16 or wider, within the bound.
No kernel may reach another device: no remote copies, remote signals or barrier semaphores. Data moves between devices by JAX's collectives and lax.ppermute only.
A program may use at most 64 MiB of HBM per device.

```python
import jax
import jax.numpy as jnp
from jax import lax

DL = 5120
DS = 1536
HD = 128
HEADS_L = 32
HEADS_S = 8
CH = 64
SEQ = 4096


def draw_latent_large(key, part):
    own_key = jax.random.fold_in(key, 1)
    noise_rows = jnp.clip(jax.random.normal(own_key, (SEQ, DL), jnp.float32), -6.0, 6.0)
    return noise_rows.astype(jnp.bfloat16)


def draw_latent_small(key, part):
    own_key = jax.random.fold_in(key, 2)
    noise_rows = jnp.clip(jax.random.normal(own_key, (SEQ, DS), jnp.float32), -6.0, 6.0)
    return noise_rows.astype(jnp.bfloat16)


def draw_qkv_large(key, part):
    own_key = jax.random.fold_in(key, 3)
    values = jnp.clip(jax.random.normal(own_key, (DL, HEADS_L * 3 * HD), jnp.float32), -6.0, 6.0) * DL ** (-0.5)
    return values.astype(jnp.bfloat16)


def draw_qkv_small(key, part):
    own_key = jax.random.fold_in(key, 4)
    values = jnp.clip(jax.random.normal(own_key, (DS, HEADS_S * 3 * HD), jnp.float32), -6.0, 6.0) * DS ** (-0.5)
    return values.astype(jnp.bfloat16)


def level_of(rng, shape, split, smallest, high):
    loudness, own = 1.0, jax.random.fold_in(rng, 6)
    for axis_at, parts in split:
        heights = jnp.exp(jax.random.uniform(jax.random.fold_in(own, axis_at), (parts,), jnp.float32, smallest / len(split), high / len(split)))
        loudness = loudness * jnp.repeat(heights, shape[axis_at] // parts).reshape([-1 if axis == axis_at else 1 for axis in range(len(shape))])
    return loudness


def gaussian(rng, shape, width, reach, split=(), held_as=jnp.bfloat16):
    entries = width * jax.random.normal(rng, shape, jnp.float32)
    if split:
        entries = entries * level_of(rng, shape, split, -0.22, 0.18)
    return jnp.clip(entries, -reach, reach).astype(held_as)


def setup_inputs(seed: int = 0) -> dict:
    seeds = jax.random.split(jax.random.key(seed), 11)
    return {
        "latent_large": draw_latent_large(jax.random.fold_in(seeds[10], 71), 0),
        "latent_small": draw_latent_small(jax.random.fold_in(seeds[10], 71), 0),
        "gain_large": jnp.clip(1.0 + 0.18 * jax.random.normal(seeds[2], (DL,), jnp.float32), 0.1, 1.9),
        "gain_small": jnp.clip(1.0 + 0.18 * jax.random.normal(seeds[3], (DS,), jnp.float32), 0.1, 1.9),
        "qkv_large": draw_qkv_large(jax.random.fold_in(seeds[10], 71), 0),
        "qkv_small": draw_qkv_small(jax.random.fold_in(seeds[10], 71), 0),
        "mix_large": gaussian(seeds[6], (HEADS_L * HD, CH), (HEADS_L * HD) ** -0.5, 0.09375, ((0, 2),)),
        "mix_small": gaussian(seeds[7], (HEADS_S * HD, CH), (HEADS_S * HD) ** -0.5, 0.1875, ((0, 2),)),
        "head_large": gaussian(seeds[8], (DL, CH), DL ** -0.5, 0.078125),
        "head_small": gaussian(seeds[9], (DS, CH), DS ** -0.5, 0.15625),
    }


GUIDANCE = 3.0
EPSILON = 1e-06

def rms_scaled(latent, gain_vec):
    values = latent.astype(jnp.float32)
    return values * lax.rsqrt(lax.optimization_barrier(jnp.mean(values * values, axis=-1, keepdims=True)) + EPSILON) * gain_vec

def attend_head(queries, keys_vals, head_dim):
    key_rows = keys_vals[:, :head_dim]
    value_rows = keys_vals[:, head_dim:]
    row_count = queries.shape[0]
    block_rows = min(512, row_count)
    blocks = queries.reshape(row_count // block_rows, block_rows, head_dim)

    def one_block(query_block):
        scores = lax.dot_general(query_block, key_rows, (((1,), (1,)), ((), ())), preferred_element_type=jnp.float32) * head_dim ** (-0.5)
        biggest = lax.optimization_barrier(jnp.max(scores, axis=1, keepdims=True))
        weights = jnp.exp(scores - biggest)
        totals = lax.optimization_barrier(jnp.sum(weights, axis=1, keepdims=True))
        mixed_rows = jnp.dot(weights.astype(jnp.bfloat16), value_rows, preferred_element_type=jnp.float32) / totals
        return mixed_rows.astype(jnp.bfloat16)
    return lax.map(one_block, blocks).reshape(row_count, head_dim)

def velocity(latent, gain_vec, qkv_weight, mix_weight, head_weight):
    head_count = mix_weight.shape[0] // HD
    row_count = latent.shape[0]
    normed = rms_scaled(latent, gain_vec).astype(jnp.bfloat16)
    projected = jnp.dot(normed, qkv_weight, preferred_element_type=jnp.float32).astype(jnp.bfloat16)
    per_head = jnp.transpose(projected.reshape(row_count, head_count, 3 * HD), (1, 0, 2))

    def one_head(columns):
        return attend_head(columns[:, :HD], columns[:, HD:], HD)
    attended = lax.map(one_head, per_head)
    attended = jnp.transpose(attended, (1, 0, 2)).reshape(row_count, head_count * HD)
    return jnp.dot(latent, head_weight, preferred_element_type=jnp.float32) + jnp.dot(attended, mix_weight, preferred_element_type=jnp.float32)

def reference(latent_large, latent_small, gain_large, gain_small, qkv_large, qkv_small, mix_large, mix_small, head_large, head_small):
    velocity_large = velocity(latent_large, gain_large, qkv_large, mix_large, head_large)
    velocity_small = velocity(latent_small, gain_small, qkv_small, mix_small, head_small)
    return velocity_small + GUIDANCE * (velocity_large - velocity_small)
```

```python
import jax
import jax.numpy as jnp
from jax import lax
from jax.sharding import Mesh, PartitionSpec as P

HD = 128
GUIDANCE = 3.0
EPSILON = 1e-06
BF = jnp.bfloat16
F32 = jnp.float32


def shift(block, axis, step):
    count = lax.axis_size(axis)
    return lax.ppermute(block, axis, [(i, (i + step) % count) for i in range(count)])


def flip(block, axis, mask):
    count = lax.axis_size(axis)
    return lax.ppermute(block, axis, [(i, i ^ mask) for i in range(count)])


def ring(block, axis):
    count = lax.axis_size(axis)
    up, down = [block], [block]
    for _ in range(count // 2 - 1):
        up.append(shift(up[-1], axis, 1))
        down.append(shift(down[-1], axis, -1))
    half = block.shape[0] // 2
    far = jnp.concatenate(
        [shift(up[-1][:half], axis, 1), shift(down[-1][half:], axis, -1)], 0
    )
    return up + [far] + down[:0:-1]


def rms_scaled(latent, gain_vec):
    values = latent.astype(F32)
    mean = jnp.mean(values * values, axis=-1, keepdims=True)
    return (values * lax.rsqrt(mean + EPSILON) * gain_vec).astype(BF)


def dot_t(rows, columns):
    return lax.dot_general(
        rows, columns, (((1,), (1,)), ((), ())), preferred_element_type=F32
    )


def attend(queries, keys, values):
    scores = dot_t(queries, keys) * HD ** (-0.5)
    weights = jnp.exp(scores - jnp.max(scores, axis=1, keepdims=True))
    totals = jnp.sum(weights, axis=1, keepdims=True)
    mixed = jnp.dot(weights.astype(BF), values, preferred_element_type=F32)
    return (mixed / totals).astype(BF)


def gather_columns(columns, x, y):
    rows, width = columns.shape
    x_low = x & 1
    cut = 2048
    buffer = jnp.zeros((2, 4, rows, width), BF)

    def put(buffer, block, which, y_at, col):
        return lax.dynamic_update_slice(buffer, block[None, None], (which, y_at, 0, col))

    first, second = columns[:, :cut], columns[:, cut:]
    pair = flip(second, "x", 1)
    near = ring(first, "y")
    rings = ring(jnp.concatenate([second, pair], 0), "y")
    sides = flip(jnp.concatenate([near[0], near[1], near[3]], 0), "x", 1)
    far = flip(near[2], "x", 1)
    other = [sides[:rows], sides[rows : 2 * rows], far, sides[2 * rows :]]
    for j in range(4):
        y_at = (y - j) % 4
        buffer = put(buffer, near[j], x_low, y_at, 0)
        buffer = put(buffer, other[j], 1 - x_low, y_at, 0)
        buffer = put(buffer, rings[j][:rows], x_low, y_at, cut)
        buffer = put(buffer, rings[j][rows:], 1 - x_low, y_at, cut)
    return buffer.reshape(8 * rows, width)


def rotated(blocks, start, axis):
    doubled = jnp.concatenate([blocks, blocks], axis)
    return lax.dynamic_slice_in_dim(doubled, start, blocks.shape[axis], axis)


def shards(
    latent_large,
    latent_small,
    gain_large,
    gain_small,
    qkv_large,
    qkv_small,
    mix_large,
    mix_small,
    head_large,
    head_small,
):
    core, z, x, y = (lax.axis_index(name) for name in ("grp", "z", "x", "y"))
    x_low, z_low = x & 1, z & 1

    latent_l = lax.dynamic_slice_in_dim(latent_large, core * 16, 16, 0)
    latent_s = lax.dynamic_slice_in_dim(latent_small, core * 16, 16, 0)
    normed_l = rms_scaled(latent_l, gain_large)
    normed_s = rms_scaled(latent_s, gain_small)

    across = lax.ppermute(normed_l, "x", [(0, 3), (3, 0), (1, 2), (2, 1)])
    rows_l = ring(jnp.concatenate([normed_l, across], 0), "z")
    rows_s = ring(normed_s, "z")
    rows_l = jnp.concatenate(rows_l[::-1], 0)
    rows_s = jnp.concatenate(rows_s[::-1], 0)

    own_l = gather_columns(qkv_large.T, x, y)
    other_l = flip(own_l, "grp", 1)
    all_s = lax.all_gather(qkv_small.T, ("grp", "x", "y"), axis=0, tiled=True)

    own_p = dot_t(rows_l, own_l).astype(BF)
    other_p = dot_t(rows_l, other_l).astype(BF)
    mine = core == x_low
    kept = jnp.where(mine, own_p, other_p)
    sent = jnp.where(mine, other_p, own_p)
    head_l = jnp.concatenate([kept, flip(sent, "x", 1)], 0)

    proj_s = dot_t(rows_s, all_s).astype(BF).reshape(8, 16, 384)
    proj_s = rotated(proj_s, 7 - z, 0).reshape(128, 384)
    first, second = proj_s[:, :192], proj_s[:, 192:]
    even = z_low == 0
    kept = jnp.where(even, first, second)
    got = flip(jnp.where(even, second, first), "z", 1)
    head_s = jnp.where(
        even, jnp.concatenate([kept, got], 1), jnp.concatenate([got, kept], 1)
    )

    pairs_l = jnp.concatenate(ring(head_l[:, HD:], "y"), 0)
    pairs_l = jnp.concatenate([pairs_l, flip(pairs_l, "grp", 1)], 0)
    pairs_s = jnp.concatenate(ring(head_s[:, HD:], "x"), 0)
    pairs_s = jnp.concatenate(ring(pairs_s, "y"), 0)
    pairs_s = jnp.concatenate([pairs_s, flip(pairs_s, "grp", 1)], 0)

    map_l = lax.dynamic_slice_in_dim(mix_large, (z * 2 + (x >> 1)) * HD, HD, 0)
    map_s = lax.dynamic_slice_in_dim(mix_small, (z >> 1) * HD, HD, 0)
    swapped = flip(jnp.concatenate([map_l, map_s], 0), "grp", 1)
    map_l = jnp.where(core == x_low, map_l, swapped[:HD])
    map_s = jnp.where(core == z_low, map_s, swapped[HD:])

    attended_l = attend(head_l[:, :HD], pairs_l[:, :HD], pairs_l[:, HD:])
    attended_s = attend(head_s[:, :HD], pairs_s[:, :HD], pairs_s[:, HD:])
    part_l = jnp.dot(attended_l, map_l, preferred_element_type=F32)
    part_s = jnp.dot(attended_s, map_s, preferred_element_type=F32)

    part_l = part_l.reshape(2, 8, 2, 16, 64)
    by_mask = jnp.stack([part_l[0, :, 0], part_l[1, :, 0], part_l[1, :, 1], part_l[0, :, 1]], 1)
    by_mask = jnp.where(x_low == 1, by_mask[:, jnp.array([1, 0, 3, 2])], by_mask)
    by_mask = jnp.where(x >= 2, by_mask[:, jnp.array([2, 3, 0, 1])], by_mask)
    by_chip = GUIDANCE * rotated(by_mask, 7 - z, 0)
    own_x = lax.broadcasted_iota(jnp.int32, (1, 4, 1, 1), 1) == x
    by_chip = by_chip + jnp.where(
        own_x, (1.0 - GUIDANCE) * part_s.reshape(8, 1, 16, 64), 0.0
    )
    returned = lax.all_to_all(
        by_chip.reshape(32, 16, 64), ("z", "x"), split_axis=0, concat_axis=0, tiled=True
    )
    direct = GUIDANCE * jnp.dot(latent_l, head_large, preferred_element_type=F32) + (
        1.0 - GUIDANCE
    ) * jnp.dot(latent_s, head_small, preferred_element_type=F32)
    half = direct + jnp.sum(returned, axis=0)
    other_half = flip(half, "grp", 1)
    return jnp.where(
        core == 0,
        jnp.concatenate([half, other_half], 0),
        jnp.concatenate([other_half, half], 0),
    )


def solution(mesh):
    grid = Mesh(mesh.devices.reshape(2, 8, 4, 4), ("grp", "z", "x", "y"))
    tokens = ("z", "x", "y")
    return jax.shard_map(
        shards,
        mesh=grid,
        in_specs=(
            P(tokens, None),
            P(tokens, None),
            P(),
            P(),
            P(None, ("grp",) + tokens),
            P(None, ("grp",) + tokens),
            P("grp", None),
            P("grp", None),
            P(),
            P(),
        ),
        out_specs=P(tokens, None),
        check_vma=False,
    )
```

```python
import functools

import jax
import jax.numpy as jnp
from jax import lax
from jax.experimental import pallas as pl
from jax.experimental.pallas import tpu as pltpu
from jax.sharding import Mesh, PartitionSpec as P

HD = 128
GUIDANCE = 3.0
EPSILON = 1e-06
BF = jnp.bfloat16
F32 = jnp.float32
KL, KS = 2560, 768
CUT = 1024
LOG2E = 1.4426950408889634
VMEM = pl.BlockSpec(memory_space=pltpu.VMEM)
SMEM = pl.BlockSpec(memory_space=pltpu.SMEM)


def shift(block, axis, step):
    count = lax.axis_size(axis)
    return lax.ppermute(block, axis, [(i, (i + step) % count) for i in range(count)])


def flip(block, axis, mask):
    count = lax.axis_size(axis)
    return lax.ppermute(block, axis, [(i, i ^ mask) for i in range(count)])


def both(block_up, block_down, axis):
    return shift(block_up, axis, 1), shift(block_down, axis, -1)


def tie(*values):
    return lax.optimization_barrier(values)


def dot_t(rows, columns):
    return lax.dot_general(
        rows, columns, (((1,), (1,)), ((), ())), preferred_element_type=F32
    )


def call(body, outs, args, specs, scratch=(), limit=32):
    return pl.pallas_call(
        body,
        out_shape=[jax.ShapeDtypeStruct(shape, dtype) for shape, dtype in outs],
        in_specs=specs,
        out_specs=[VMEM] * len(outs),
        scratch_shapes=list(scratch),
        compiler_params=pltpu.CompilerParams(vmem_limit_bytes=limit * 2**20),
    )(*args)


def norm_body(where, large, small, gain_l, gain_s, out_l, out_s):
    core = where[0]
    for latent, gain, out, width in ((large, gain_l, out_l, KL), (small, gain_s, out_s, KS)):
        values = latent[...].astype(F32)
        mean = jnp.mean(values * values, axis=-1, keepdims=True)
        at = pl.ds(pl.multiple_of(core * width, width), width)
        half = latent[:, at].astype(F32)
        out[...] = (half * lax.rsqrt(mean + EPSILON) * gain[:, at]).astype(BF)


def project_body(*refs):
    (where, near, across, up1, up2, up3, down1, down2, down3, far_up, far_down) = refs[:11]
    (s_own, s_up, s_down) = refs[11:14]
    wa, wb, ya_up, ya_down, yb_up, yb_down, f_up, f_down = refs[14:22]
    xb, xa, xa_up, xa_down, xa_far, yp_up, yp_down, p_up, p_down, ws4 = refs[22:32]
    keep_l, send_l, keep_s, send_s = refs[32:36]
    rows, cols, rows_s, cols_s = refs[36:40]
    core = where[0]
    halves = (
        pl.ds(pl.multiple_of(core * 16, 16), 16),
        pl.ds(pl.multiple_of((1 - core) * 16, 16), 16),
    )
    pair_halves = (
        pl.ds(pl.multiple_of(core * 16 + 32, 16), 16),
        pl.ds(pl.multiple_of((1 - core) * 16 + 32, 16), 16),
    )
    wide = slice(0, KL)
    for h in range(2):
        base = 256 * h
        for k, ref in ((0, down1), (1, down2), (2, down3), (4, up3), (5, up2), (6, up1)):
            rows[base + 32 * k : base + 32 * k + 16, :] = ref[halves[h], wide]
            rows[base + 32 * k + 16 : base + 32 * k + 32, :] = ref[pair_halves[h], wide]
        rows[base + 96 : base + 112, :] = far_up[halves[h], :]
        rows[base + 112 : base + 128, :] = far_down[halves[h], :]
        rows[base + 224 : base + 240, :] = near[halves[h], :]
        rows[base + 240 : base + 256, :] = across[halves[h], :]
        base = 128 * h
        for k, ref in ((0, s_down), (6, s_up), (7, s_own)):
            rows_s[base + 16 * k : base + 16 * k + 16, :] = ref[halves[h], :]
        for k, ref in ((1, down1), (2, down2), (3, up3), (4, up2), (5, up1)):
            at = slice(base + 16 * k, base + 16 * k + 16)
            rows_s[at, : KS // 2] = ref[halves[h], KL:]
            rows_s[at, KS // 2 :] = ref[pair_halves[h], KL:]
    for h in range(2):
        src = slice(48 * h, 48 * h + 48)

        def put(block, col, ref, lo, hi):
            at = 384 * h + 48 * block
            cols[at : at + 48, col : col + hi - lo] = ref[src, lo:hi]

        put(0, 0, wa, 0, CUT)
        put(0, CUT, wb, 0, KL - CUT)
        put(1, 0, ya_up, 0, CUT)
        put(1, CUT, yb_up, 0, KL - CUT)
        put(2, 0, f_up, 0, KL // 2)
        put(2, KL // 2, f_down, 0, KL // 2)
        put(3, 0, ya_down, 0, CUT)
        put(3, CUT, yb_down, 0, KL - CUT)
        put(4, 0, xa, 0, CUT)
        put(4, CUT, xb, 0, KL - CUT)
        put(5, 0, xa_up, 0, CUT)
        put(5, CUT, yp_up, 0, KL - CUT)
        put(6, 0, xa_far, 0, CUT)
        put(6, CUT, p_up, 0, 1152)
        put(6, CUT + 1152, p_down, 0, 384)
        put(7, 0, xa_down, 0, CUT)
        put(7, CUT, yp_down, 0, KL - CUT)
    cols_s[0:96, :] = ws4[...]
    cols_s[96:192, :] = yp_up[:, KL - CUT :]
    cols_s[192:288, :] = p_down[:, 384:]
    cols_s[288:384, :] = yp_down[:, KL - CUT :]

    small = dot_t(rows_s[...], cols_s[...])
    keep_s[...] = small[:128]
    send_s[...] = small[128:]

    @pl.loop(0, 3)
    def _(n):
        at = pl.ds(pl.multiple_of(n * 256, 256), 256)
        block = dot_t(rows[...], cols[at, :])
        keep_l[:, at] = block[:256]
        send_l[:, at] = block[256:]


def order_body(where, keep_l, got_l, keep_s, got_s, order_l, order_s, kept, sent, kept_s, sent_s):
    core, z, x = where[0], where[1], where[2]
    own = (keep_l[:, :384] + got_l[:, 384:]).astype(BF)
    other = (keep_l[:, 384:] + got_l[:, :384]).astype(BF)
    mine = core == x % 2
    first = jnp.where(mine, own, other)
    second = jnp.where(mine, other, own)
    for value, out in ((first, kept), (second, sent)):
        value = jnp.dot(value, order_l[...], preferred_element_type=F32).astype(BF)
        for k in range(8):
            z_at = (z + 1 + k) % 8
            at = pl.ds(pl.multiple_of(z_at * 32, 32), 32)
            out[at, :] = value[32 * k : 32 * k + 32]
    total = keep_s[...]
    value = (total + got_s[...]).astype(BF)
    value = jnp.dot(value, order_s[...], preferred_element_type=F32).astype(BF)
    for k in range(8):
        z_at = (z + 1 + k) % 8
        at = pl.ds(pl.multiple_of(z_at * 16, 16), 16)
        kept_s[at, :] = value[16 * k : 16 * k + 16, :256]
        sent_s[at, :] = value[16 * k : 16 * k + 16, 256:]


def attend(query, pairs, scores):
    top = None
    start = 0
    for ref in pairs:
        count = ref.shape[0]
        block = dot_t(query, ref[:, :HD])
        scores[:, start : start + count] = block
        for at in range(0, count, 128):
            part = block[:, at : at + 128]
            top = part if top is None else jnp.maximum(top, part)
        start += count
    biggest = jnp.max(top, axis=1, keepdims=True)
    total, mixed = None, None
    start = 0
    for ref in pairs:
        count = ref.shape[0]
        block = scores[:, start : start + count]
        weights = jnp.exp2((block - biggest) * (HD**-0.5 * LOG2E))
        for at in range(0, count, 128):
            part = weights[:, at : at + 128]
            total = part if total is None else total + part
        term = jnp.dot(weights.astype(BF), ref[:, HD:], preferred_element_type=F32)
        mixed = term if mixed is None else mixed + term
        start += count
    return (mixed / jnp.sum(total, axis=1, keepdims=True)).astype(BF)


def large_body(where, query, map_left, map_right, *refs):
    pairs, out, scores = refs[:10], refs[10], refs[11]
    x = where[2]

    @pl.loop(0, 2)
    def _(s):
        done = attend(query[pl.ds(pl.multiple_of(s * 256, 256), 256), :], pairs, scores)
        left = jnp.dot(done, map_left[...], preferred_element_type=F32)
        right = jnp.dot(done, map_right[...], preferred_element_type=F32)
        x_first = x ^ s
        for z in range(8):
            for p in range(2):
                x_at = x_first ^ (3 * p)
                row = z * 32 + p * 16
                out[z * 4 + x_at] = GUIDANCE * (left[row : row + 8] + right[row + 8 : row + 16])


def small_body(where, query, map_left, map_right, big, *refs):
    pairs, out, scores = refs[:10], refs[10], refs[11]
    x = where[2]
    done = attend(query[...], pairs, scores)
    left = jnp.dot(done, map_left[...], preferred_element_type=F32)
    right = jnp.dot(done, map_right[...], preferred_element_type=F32)
    out[...] = big[...]
    for z in range(8):
        row = z * 16
        out[z * 4 + x] += (1.0 - GUIDANCE) * (left[row : row + 8] + right[row + 8 : row + 16])


def shards(
    latent_large,
    latent_small,
    gain_large,
    gain_small,
    qkv_large,
    qkv_small,
    mix_large,
    mix_small,
    head_large,
    head_small,
):
    core, z, x, y = (lax.axis_index(name) for name in ("grp", "z", "x", "y"))
    x_low, z_low = x & 1, z & 1
    where = jnp.stack([core, z, x, y])
    opposite = [(0, 3), (3, 0), (1, 2), (2, 1)]

    def halves(columns, width):
        own = lax.dynamic_slice_in_dim(columns, core * width, width, 1)
        other = lax.dynamic_slice_in_dim(columns, (1 - core) * width, width, 1)
        return jnp.concatenate([own, flip(other, "grp", 1)], 0)

    w = halves(qkv_large.T, KL)
    ws = halves(qkv_small.T, KS)
    wa, wb = w[:, :CUT], w[:, CUT:]

    near, s_own = call(
        norm_body,
        [((32, KL), BF), ((32, KS), BF)],
        (where, latent_large, latent_small, gain_large[None], gain_small[None]),
        [SMEM] + [VMEM] * 4,
    )

    across = lax.ppermute(near, "x", opposite)
    s_up, s_down = both(s_own, s_own, "z")
    xb = flip(wb, "x", 1)
    ya_up, ya_down = both(wa, wa, "y")
    ws_far = lax.ppermute(ws, "x", opposite)

    def packed(small):
        small = jnp.concatenate([small[:, : KS // 2], small[:, KS // 2 :]], 0)
        return jnp.concatenate([jnp.concatenate([near, across], 0), small], 1)

    up1, down1 = both(packed(s_up), packed(s_down), "z")
    wb1, wa1, ws_far, ya_up, ya_down, _ = tie(wb, wa, ws_far, ya_up, ya_down, across)
    yb_up, yb_down = both(wb1, wb1, "y")
    ws2 = jnp.concatenate([ws, ws_far], 0)
    xa = flip(jnp.concatenate([wa1, jnp.concatenate([ws2, ws2], 0)], 1), "x", 1)

    up2, down2 = both(up1, down1, "z")
    xb2, xa, ya_up, ya_down, yb_up, yb_down, _, _ = tie(
        xb, xa, ya_up, ya_down, yb_up, yb_down, up1, down1
    )
    ws4 = jnp.concatenate([ws2, xa[:48, CUT:]], 0)
    yp = jnp.concatenate([xb2, ws4], 1)
    yp_up, yp_down = both(yp, yp, "y")
    xa_up = flip(ya_up, "x", 1)

    up3, down3 = both(up2, down2, "z")
    ya_down, yp_up, yp_down, xa_up, yb_up, yb_down, _, _ = tie(
        ya_down, yp_up, yp_down, xa_up, yb_up, yb_down, up2, down2
    )
    f_up, f_down = both(
        jnp.concatenate([ya_up, yb_up[:, : KL // 2 - CUT]], 1), yb_down[:, KL // 2 - CUT :], "y"
    )
    xa_down = flip(ya_down, "x", 1)

    far_up, far_down = both(up3[:32, :KL], down3[32:, :KL], "z")
    f_up, yp_up, yp_down, xa_down, _, _ = tie(f_up, yp_up, yp_down, xa_down, up3, down3)
    p_up, p_down = both(yp_up[:, :1152], yp_down[:, 1152:], "y")
    xa_far = flip(f_up[:, :CUT], "x", 1)

    keep_l, send_l, keep_s, send_s = call(
        project_body,
        [((256, 768), F32)] * 2 + [((128, 384), F32)] * 2,
        (
            where, near, across, up1, up2, up3, down1, down2, down3, far_up, far_down,
            s_own, s_up, s_down,
            wa, wb, ya_up, ya_down, yb_up, yb_down, f_up, f_down,
            xb, xa, xa_up, xa_down, xa_far, yp_up, yp_down, p_up, p_down, ws4,
        ),
        [SMEM] + [VMEM] * 31,
        [
            pltpu.VMEM((512, KL), BF),
            pltpu.VMEM((768, KL), BF),
            pltpu.VMEM((256, KS), BF),
            pltpu.VMEM((384, KS), BF),
        ],
        limit=40,
    )
    got_l = flip(send_l, "grp", 1)
    got_s = flip(send_s, "grp", 1)

    source = lax.broadcasted_iota(jnp.int32, (384, 384), 0)
    target = lax.broadcasted_iota(jnp.int32, (384, 384), 1)
    block = target // 48
    from_l = jnp.where(block // 4 == x_low, 0, 4) + ((y - block) & 3)
    order_l = (source == from_l * 48 + target % 48).astype(BF)
    half = target // 192
    wanted = jnp.where(half == 0, z_low, 1 - z_low)
    within = target % 192
    piece = within // 12
    mask = (piece // 4) ^ x
    x_group = jnp.where(mask == 0, 0, jnp.where(mask == 3, 1, jnp.where(mask == 1, 2, 3)))
    from_s = ((y - piece) & 3) * 96 + x_group * 24 + jnp.where(wanted == core, 0, 12) + within % 12
    order_s = (source == from_s).astype(BF)
    return_s = got_s.reshape(128, 16, 2, 12)[:, :, ::-1].reshape(128, 384)
    order_s = jnp.concatenate(
        [order_s[:, :192], jnp.zeros((384, 64), BF), order_s[:, 192:], jnp.zeros((384, 64), BF)], 1
    )

    kept, sent, kept_s, sent_s = call(
        order_body,
        [((256, 384), BF)] * 2 + [((128, 256), BF)] * 2,
        (where, keep_l, got_l, keep_s, return_s, order_l, order_s),
        [SMEM] + [VMEM] * 6,
    )

    taken = flip(sent, "x", 1)
    taken_s = flip(sent_s[:, :192], "z", 1)
    kept_s = kept_s[:, :192]
    head_s = jnp.where(
        z_low == 0,
        jnp.concatenate([kept_s, taken_s], 1),
        jnp.concatenate([taken_s, kept_s], 1),
    )
    query_l = jnp.concatenate([kept[:, :HD], taken[:, :HD]], 0)
    own_l = jnp.concatenate([kept[:, HD:], taken[:, HD:]], 0)
    own_s = head_s[:, HD:]

    k_up, k_down = both(own_l, own_l, "y")
    c_own = flip(own_l, "grp", 1)
    beside = [flip(own_s, "x", 1), lax.ppermute(own_s, "x", opposite), flip(own_s, "x", 2)]
    own_s = jnp.concatenate([own_s] + beside, 0)
    own_s, k_up, k_down = tie(own_s, k_up, k_down)

    k_far_up, k_far_down = both(k_up[:256], k_down[256:], "y")
    c_up, c_down = flip(k_up, "grp", 1), flip(k_down, "grp", 1)
    ks_up, ks_down = both(own_s, own_s, "y")
    cs_own = flip(own_s, "grp", 1)
    k_far_up, k_far_down, ks_up, ks_down = tie(k_far_up, k_far_down, ks_up, ks_down)

    c_far_up, c_far_down = flip(k_far_up, "grp", 1), flip(k_far_down, "grp", 1)
    ks_far_up, ks_far_down = both(ks_up[:256], ks_down[256:], "y")
    cs_up, cs_down = flip(ks_up, "grp", 1), flip(ks_down, "grp", 1)

    map_l = lax.dynamic_slice_in_dim(mix_large, (z * 2 + (x >> 1)) * HD, HD, 0)
    map_s = lax.dynamic_slice_in_dim(mix_small, (z >> 1) * HD, HD, 0)
    swapped = flip(jnp.concatenate([map_l, map_s], 0), "grp", 1)
    map_l = jnp.where(core == x_low, map_l, swapped[:HD])
    map_s = jnp.where(core == z_low, map_s, swapped[HD:])
    blank = jnp.zeros((HD, 64), BF)

    def sides(values):
        return jnp.concatenate([values, blank], 1), jnp.concatenate([blank, values], 1)

    (big,) = call(
        large_body,
        [((32, 8, 128), F32)],
        (where, query_l, *sides(map_l), own_l, k_up, k_down, k_far_up, k_far_down)
        + (c_own, c_up, c_down, c_far_up, c_far_down),
        [SMEM] + [VMEM] * 13,
        [pltpu.VMEM((256, 4096), F32)],
    )
    cs_far_up, cs_far_down = flip(ks_far_up, "grp", 1), flip(ks_far_down, "grp", 1)
    (big,) = call(
        small_body,
        [((32, 8, 128), F32)],
        (where, head_s[:, :HD], *sides(map_s), big, own_s, ks_up, ks_down, ks_far_up, ks_far_down)
        + (cs_own, cs_up, cs_down, cs_far_up, cs_far_down),
        [SMEM] + [VMEM] * 14,
        [pltpu.VMEM((128, 4096), F32)],
    )

    returned = lax.all_to_all(big, ("z", "x"), split_axis=0, concat_axis=0, tiled=True)
    returned = jnp.sum(returned, axis=0)
    latent_l = lax.dynamic_slice_in_dim(latent_large, core * 16, 16, 0)
    latent_s = lax.dynamic_slice_in_dim(latent_small, core * 16, 16, 0)
    direct = GUIDANCE * jnp.dot(latent_l, head_large, preferred_element_type=F32) + (
        1.0 - GUIDANCE
    ) * jnp.dot(latent_s, head_small, preferred_element_type=F32)
    part = direct + jnp.concatenate([returned[:, :64], returned[:, 64:]], 0)
    other_part = flip(part, "grp", 1)
    return jnp.where(
        core == 0,
        jnp.concatenate([part, other_part], 0),
        jnp.concatenate([other_part, part], 0),
    )


def solution(mesh):
    grid = Mesh(mesh.devices.reshape(2, 8, 4, 4), ("grp", "z", "x", "y"))
    tokens = ("z", "x", "y")
    return jax.shard_map(
        shards,
        mesh=grid,
        in_specs=(
            P(tokens, None),
            P(tokens, None),
            P(),
            P(),
            P(None, ("grp",) + tokens),
            P(None, ("grp",) + tokens),
            P("grp", None),
            P("grp", None),
            P(),
            P(),
        ),
        out_specs=P(tokens, None),
        check_vma=False,
    )
```

```python
import jax
import jax.numpy as jnp
from jax import lax
from jax.experimental import pallas as pl
from jax.experimental.pallas import tpu as pltpu
from jax.sharding import Mesh, PartitionSpec as P

HD = 128
GUIDANCE = 3.0
EPSILON = 1e-06
BF = jnp.bfloat16
F32 = jnp.float32
DL, DS = 5120, 1536
CUT = 1536
PART = 512
WA = CUT + 2 * PART
WB = DL - CUT
LOG2E = 1.4426950408889634
VMEM = pl.BlockSpec(memory_space=pltpu.VMEM)
SMEM = pl.BlockSpec(memory_space=pltpu.SMEM)
OPPOSITE = [(0, 3), (3, 0), (1, 2), (2, 1)]


def flip(block, axis, mask):
    count = lax.axis_size(axis)
    return lax.ppermute(block, axis, [(i, i ^ mask) for i in range(count)])


def swap(block):
    return flip(block, "grp", 1)


def cross(block):
    return lax.ppermute(block, "x", OPPOSITE)


def spread(block, axis):
    n = lax.axis_size(axis)
    pairs = [(i, (i + 1) % n) for i in range(n)]
    pairs += [(n + i, n + (i - 1) % n) for i in range(n)]
    return lax.ppermute(block, ("grp", axis), pairs)


def tie(*values):
    return lax.optimization_barrier(values)


def dot_t(rows, columns):
    return lax.dot_general(
        rows, columns, (((1,), (1,)), ((), ())), preferred_element_type=F32
    )


def call(body, outs, args, scratch=(), limit=16):
    return pl.pallas_call(
        body,
        out_shape=[jax.ShapeDtypeStruct(shape, dtype) for shape, dtype in outs],
        in_specs=[SMEM] + [VMEM] * (len(args) - 1),
        out_specs=[VMEM] * len(outs),
        scratch_shapes=list(scratch),
        compiler_params=pltpu.CompilerParams(vmem_limit_bytes=limit * 2**20),
    )(*args)


def norm_body(where, large, small, gain_l, gain_s, out):
    for latent, gain, at, width in ((large, gain_l, 0, DL), (small, gain_s, DL, DS)):
        values = latent[...].astype(F32)
        mean = jnp.mean(values * values, axis=-1, keepdims=True)
        out[:, at : at + width] = (values * lax.rsqrt(mean + EPSILON) * gain[...]).astype(BF)


def project_body(*refs):
    (where, near, across, z1, z2, z3, zf, f1, f2, f3, ff, s_got) = refs[:12]
    (a0, b0, ay, ay_g, by, by_g, fo, fo_g) = refs[12:20]
    (xa, xa_g, xb, xb_g, xay, xay_g, yp, yp_g, xaf, xaf_g, pf, pf_g) = refs[20:32]
    order_l, order_s = refs[32:34]
    kept, sent, kept_s, sent_s = refs[34:38]
    rows, cols, rows_s, cols_s, result = refs[38:43]
    core, z, x = where[0], where[1], where[2]

    rows[0:32, :] = jnp.where(core == 0, near[:, :DL], across[...])
    for i, (own, pair) in enumerate(((z1, f1), (z2, f2), (z3, f3))):
        rows[32 + 64 * i : 64 + 64 * i, :] = own[:, :DL]
        rows[64 + 64 * i : 96 + 64 * i, :] = pair[...]
    rows[224:240, :] = zf[:, :DL]
    rows[240:256, :] = ff[...]

    half = pl.ds(pl.multiple_of(core * 16, 16), 16)
    way = 2 * core - 1

    def at_z(step):
        return pl.ds(pl.multiple_of((z + 8 + step) % 8 * 16, 16), 16)

    rows_s[at_z(0), :] = near[half, DL:]
    rows_s[at_z(4), :] = zf[:, DL:]
    for i, own in ((1, z1), (2, z2), (3, z3)):
        rows_s[at_z(way * i), :] = own[half, DL:]
        rows_s[at_z(-way * i), :] = s_got[16 * i - 16 : 16 * i, :]

    def put(group, block, row, a_ref, a_col, b_ref, b_col):
        at = 384 * group + 48 * block
        cols[at : at + 48, :CUT] = a_ref[row : row + 48, a_col : a_col + CUT]
        cols[at : at + 48, CUT:] = b_ref[row : row + 48, b_col : b_col + WB]
        for side in range(2):
            base = (group * 16 + block * 2 + side) * 16
            col = a_col + CUT + PART * side
            for q in range(3):
                cols_s[base : base + 16, q * PART : q * PART + PART] = a_ref[
                    row + 16 * q : row + 16 * q + 16, col : col + PART
                ]

    for group in range(2):
        row, turned = 48 * group, 48 * (1 - group)
        far, far_x, far_p = ((fo, xaf, pf), (fo_g, xaf_g, pf_g))[group]
        pair_a, pair_b = ((xa, xb), (xa_g, xb_g))[group]
        put(group, 0, row, a0, 0, b0, 0)
        put(group, 1, row, ay, 0, by, 0)
        put(group, 2, 0, far, 0, far, WA)
        put(group, 3, turned, ay_g, 0, by_g, 0)
        put(group, 4, 0, pair_a, 0, pair_b, 0)
        put(group, 5, row, xay, 0, yp, 0)
        put(group, 6, 0, far_x, 0, far_p, 0)
        put(group, 7, turned, xay_g, 0, yp_g, 0)

    small = dot_t(rows_s[...], cols_s[...]).astype(BF)
    small = jnp.dot(small, order_s[...], preferred_element_type=F32).astype(BF)
    kept_s[...] = small[:, :256]
    sent_s[...] = small[:, 256:]

    @pl.loop(0, 3)
    def _(n):
        at = pl.ds(pl.multiple_of(n * 256, 256), 256)
        result[:, at] = dot_t(rows[...], cols[at, :]).astype(BF)

    own, other = result[:, :384], result[:, 384:]
    mine = core == x % 2
    for value, out in ((jnp.where(mine, own, other), kept), (jnp.where(mine, other, own), sent)):
        out[...] = jnp.dot(value, order_l[...], preferred_element_type=F32).astype(BF)


def attend(query, pairs, scores):
    top = None
    start = 0
    for ref in pairs:
        for lo in range(0, ref.shape[0], 512):
            count = min(512, ref.shape[0] - lo)
            block = dot_t(query, ref[lo : lo + count, :HD])
            scores[:, start : start + count] = block
            for at in range(0, count, 128):
                part = block[:, at : at + 128]
                top = part if top is None else jnp.maximum(top, part)
            start += count
    biggest = jnp.max(top, axis=1, keepdims=True)
    total, mixed = None, None
    start = 0
    for ref in pairs:
        for lo in range(0, ref.shape[0], 512):
            count = min(512, ref.shape[0] - lo)
            block = scores[:, start : start + count]
            weights = jnp.exp2((block - biggest) * (HD**-0.5 * LOG2E))
            for at in range(0, count, 128):
                part = weights[:, at : at + 128]
                total = part if total is None else total + part
            values = ref[lo : lo + count, HD:]
            term = jnp.dot(weights.astype(BF), values, preferred_element_type=F32)
            mixed = term if mixed is None else mixed + term
            start += count
    return (mixed / jnp.sum(total, axis=1, keepdims=True)).astype(BF)


def large_body(where, query, map_left, map_right, *refs):
    pairs, out, scores = refs[:-2], refs[-2], refs[-1]
    core, z, x = where[0], where[1], where[2]
    way = 2 * core - 1
    out[...] = jnp.zeros_like(out)

    @pl.loop(0, 2)
    def _(s):
        done = attend(query[pl.ds(pl.multiple_of(s * 256, 256), 256), :], pairs, scores)
        left = GUIDANCE * jnp.dot(done, map_left[...], preferred_element_type=F32)
        right = GUIDANCE * jnp.dot(done, map_right[...], preferred_element_type=F32)
        x_own = x ^ s

        def chip(step, x_at):
            return (z + 8 + step) % 8 * 4 + x_at

        def place(to, row):
            out[to] = left[row : row + 16] + right[row + 16 : row + 32]

        place(chip(0, x_own ^ (3 * core)), 0)
        for i in range(1, 4):
            place(chip(way * i, x_own), 64 * i - 32)
            place(chip(way * i, x_own ^ 3), 64 * i)
        out[chip(4, x_own)] = jnp.where(core == 0, left[224:240], right[224:240])
        out[chip(4, x_own ^ 3)] = jnp.where(core == 0, left[240:256], right[240:256])


def small_body(where, query, map_left, map_right, big, *refs):
    pairs, out, scores = refs[:-2], refs[-2], refs[-1]
    core, x = where[0], where[2]
    done = attend(query[...], pairs, scores)
    side = jnp.where(core == 0, map_left[...], map_right[...])
    part = (1.0 - GUIDANCE) * jnp.dot(done, side, preferred_element_type=F32)
    out[...] = big[...]
    for z in range(8):
        out[z * 4 + x] += part[16 * z : 16 * z + 16]


def shards(
    latent_large,
    latent_small,
    gain_large,
    gain_small,
    qkv_large,
    qkv_small,
    mix_large,
    mix_small,
    head_large,
    head_small,
):
    core, z, x, y = (lax.axis_index(name) for name in ("grp", "z", "x", "y"))
    x_low, z_low = x & 1, z & 1
    where = jnp.stack([core, z, x, y])

    w = qkv_large.T
    ws = jnp.concatenate([qkv_small.T, jnp.zeros((4, DS), BF)], 0)
    ws = jnp.concatenate([ws[:, :PART], ws[:, PART : 2 * PART], ws[:, 2 * PART :]], 0)
    w_b = w[:, CUT:]
    xb = flip(w_b, "x", 1)
    ws_cross = cross(ws)
    b0 = jnp.concatenate([w_b, swap(w_b)], 0)

    (near,) = call(
        norm_body,
        [((32, DL + DS), BF)],
        (where, latent_large, latent_small, gain_large[None], gain_small[None]),
    )
    z1 = spread(near, "z")
    across = lax.ppermute(near[:, :DL], ("grp", "x"), [(4 + i, 4 + j) for i, j in OPPOSITE])

    by = spread(b0, "y")
    own_a = jnp.concatenate([w[:, :CUT], ws, ws_cross], 1)
    a0 = jnp.concatenate([own_a, swap(own_a)], 0)
    ay = spread(a0, "y")
    xa = flip(own_a, "x", 1)

    z2 = spread(z1, "z")
    f1 = cross(z1[:, :DL])
    xb, _ = tie(xb, z1)
    xb_g = swap(xb)
    yp = spread(jnp.concatenate([xb, xb_g], 0), "y")

    z3 = spread(z2, "z")
    f2 = cross(z2[:, :DL])
    ay, by, xa, _ = tie(ay, by, xa, z2)
    ay_g, by_g, xa_g = swap(ay), swap(by), swap(xa)
    xay = flip(ay, "x", 1)
    fo = spread(jnp.concatenate([ay[:48], by[:48]], 1), "y")

    zf = spread(lax.dynamic_slice_in_dim(z3, core * 16, 16, 0), "z")
    f3 = cross(z3[:, :DL])
    yp, xay, fo, _ = tie(yp, xay, fo, z3)
    yp_g, xay_g, fo_g = swap(yp), swap(xay), swap(fo)
    pf = spread(yp[:48], "y")
    xaf = flip(fo[:, :WA], "x", 1)
    others = (1 - core) * 16
    s_got = swap(
        jnp.concatenate([lax.dynamic_slice(v, (others, DL), (16, DS)) for v in (z1, z2, z3)], 0)
    )

    ff = cross(zf[:, :DL])
    pf_g, xaf_g = swap(pf), swap(xaf)

    def position(y_at):
        away = (y - y_at) & 3
        return jnp.where((away & 1 == 1) & (core == 1), 4 - away, away)

    source = lax.broadcasted_iota(jnp.int32, (384, 384), 0)
    target = lax.broadcasted_iota(jnp.int32, (384, 384), 1)
    block = target // 48
    from_l = jnp.where(block // 4 == x_low, 0, 4) + position(block & 3)
    order_l = (source == from_l * 48 + target % 48).astype(BF)
    source = lax.broadcasted_iota(jnp.int32, (512, 512), 0)
    target = lax.broadcasted_iota(jnp.int32, (512, 512), 1)
    group = jnp.where((target // 256 == 0) == (core == z_low), 0, 1)
    within = target % 256
    piece = within // 12
    mask = ((piece // 4) & 3) ^ x
    side = jnp.where((mask == 0) | (mask == 1), 0, 1)
    pair = jnp.where((mask == 0) | (mask == 3), 0, 4)
    from_s = (group * 16 + (pair + position(piece & 3)) * 2 + side) * 16 + within % 12
    order_s = ((source == from_s) & (within < 192)).astype(BF)

    kept, sent, kept_s, sent_s = call(
        project_body,
        [((256, 384), BF)] * 2 + [((128, 256), BF)] * 2,
        (
            where, near, across, z1, z2, z3, zf, f1, f2, f3, ff, s_got,
            a0, b0, ay, ay_g, by, by_g, fo, fo_g,
            xa, xa_g, xb, xb_g, xay, xay_g, yp, yp_g, xaf, xaf_g, pf, pf_g,
            order_l, order_s,
        ),
        [
            pltpu.VMEM((256, DL), BF),
            pltpu.VMEM((768, DL), BF),
            pltpu.VMEM((128, DS), BF),
            pltpu.VMEM((512, DS), BF),
            pltpu.VMEM((256, 768), BF),
        ],
        limit=20,
    )

    taken = flip(sent, "x", 1)
    taken_s = flip(sent_s, "z", 1)
    query_l = jnp.concatenate([kept[:, :HD], taken[:, :HD]], 0)
    own_l = jnp.concatenate([kept[:, HD:], taken[:, HD:]], 0)
    got_l = swap(own_l)
    k_side = spread(jnp.concatenate([own_l, got_l], 0), "y")

    kept_s, taken_s = kept_s[:, :192], taken_s[:, :192]
    head_s = jnp.where(
        z_low == 0,
        jnp.concatenate([kept_s, taken_s], 1),
        jnp.concatenate([taken_s, kept_s], 1),
    )
    own_s = head_s[:, HD:]
    got_s = swap(own_s)
    chip_s = jnp.concatenate([own_s, got_s], 0)
    x1 = spread(chip_s, "x")
    x2 = flip(own_s, "x", 2)
    x1, x2, k_side = tie(x1, x2, k_side)

    k_far = spread(k_side[:512], "y")
    k_side_g = swap(k_side)
    x1_g, x2_g = swap(x1), swap(x2)
    all_s = jnp.concatenate(
        [own_s, x1[:128], x1_g[128:], x2, got_s, x1[128:], x1_g[:128], x2_g], 0
    )
    k_far, all_s = tie(k_far, all_s)
    k_far_g = swap(k_far)
    s_side = spread(all_s, "y")

    map_l = lax.dynamic_slice_in_dim(mix_large, (z * 2 + (x >> 1)) * HD, HD, 0)
    map_s = lax.dynamic_slice_in_dim(mix_small, (z >> 1) * HD, HD, 0)
    swapped = swap(jnp.concatenate([map_l, map_s], 0))
    map_l = jnp.where(core == x_low, map_l, swapped[:HD])
    map_s = jnp.where(core == z_low, map_s, swapped[HD:])
    blank = jnp.zeros((HD, 64), BF)

    def sides(values):
        return jnp.concatenate([values, blank], 1), jnp.concatenate([blank, values], 1)

    (big,) = call(
        large_body,
        [((32, 16, 128), F32)],
        (where, query_l, *sides(map_l), own_l, got_l, k_side, k_side_g, k_far, k_far_g),
        [pltpu.VMEM((256, 4096), F32)],
    )
    s_far = spread(s_side[:512], "y")
    s_side_g = swap(s_side)
    s_far_g = swap(s_far)
    (big,) = call(
        small_body,
        [((32, 16, 128), F32)],
        (where, head_s[:, :HD], *sides(map_s), big, all_s, s_side, s_side_g, s_far, s_far_g),
        [pltpu.VMEM((128, 4096), F32)],
    )

    returned = lax.all_to_all(big, ("z", "x"), split_axis=0, concat_axis=0, tiled=True)
    part = jnp.sum(returned, axis=0)
    total = part + swap(part)
    direct = GUIDANCE * jnp.dot(latent_large, head_large, preferred_element_type=F32) + (
        1.0 - GUIDANCE
    ) * jnp.dot(latent_small, head_small, preferred_element_type=F32)
    return direct + jnp.concatenate([total[:, :64], total[:, 64:]], 0)


def solution(mesh):
    grid = Mesh(mesh.devices.reshape(2, 8, 4, 4), ("grp", "z", "x", "y"))
    tokens = ("z", "x", "y")
    return jax.shard_map(
        shards,
        mesh=grid,
        in_specs=(
            P(tokens, None),
            P(tokens, None),
            P(),
            P(),
            P(None, ("grp",) + tokens),
            P(None, ("grp",) + tokens),
            P("grp", None),
            P("grp", None),
            P(),
            P(),
        ),
        out_specs=P(tokens, None),
        check_vma=False,
    )
```

```python
import jax
import jax.numpy as jnp
from jax import lax
from jax.experimental import pallas as pl
from jax.experimental.pallas import tpu as pltpu
from jax.sharding import Mesh, PartitionSpec as P

HD = 128
GUIDANCE = 3.0
EPSILON = 1e-06
BF = jnp.bfloat16
F32 = jnp.float32
DL, DS = 5120, 1536
KS = DS // 2
PART = 512
LOG2E = 1.4426950408889634
VMEM = pl.BlockSpec(memory_space=pltpu.VMEM)
SMEM = pl.BlockSpec(memory_space=pltpu.SMEM)
ANY = pl.BlockSpec(memory_space=pl.ANY)
OPPOSITE = [(0, 3), (3, 0), (1, 2), (2, 1)]


def flip(block, axis, mask):
    count = lax.axis_size(axis)
    return lax.ppermute(block, axis, [(i, i ^ mask) for i in range(count)])


def swap(block):
    return flip(block, "grp", 1)


def cross(block):
    return lax.ppermute(block, "x", OPPOSITE)


def spread(block, axis):
    n = lax.axis_size(axis)
    pairs = [(i, (i + 1) % n) for i in range(n)]
    pairs += [(n + i, n + (i - 1) % n) for i in range(n)]
    return lax.ppermute(block, ("grp", axis), pairs)


def tie(*values):
    return lax.optimization_barrier(values)


def dot_t(rows, columns):
    return lax.dot_general(
        rows, columns, (((1,), (1,)), ((), ())), preferred_element_type=F32
    )


def call(body, outs, args, scratch=(), limit=16, placed=None, flops=0):
    return pl.pallas_call(
        body,
        out_shape=[jax.ShapeDtypeStruct(shape, dtype) for shape, dtype in outs],
        in_specs=placed or [SMEM] + [VMEM] * (len(args) - 1),
        out_specs=[VMEM] * len(outs),
        scratch_shapes=list(scratch),
        compiler_params=pltpu.CompilerParams(vmem_limit_bytes=limit * 2**20),
        cost_estimate=pl.CostEstimate(flops=flops, bytes_accessed=2**20, transcendentals=0),
    )(*args)


def norm_body(where, large, small, gain_l, gain_s, mine, other, out_s, hold_l, hold_s, g_l, g_s, sems):
    core = where[0]
    tasks = [
        pltpu.make_async_copy(source, target, sems.at[i])
        for i, (source, target) in enumerate(
            ((large, hold_l), (small, hold_s), (gain_l, g_l), (gain_s, g_s))
        )
    ]
    for task in tasks:
        task.start()
    for task in tasks:
        task.wait()

    def normed(latent, gain, half, width):
        values = latent[pl.ds(pl.multiple_of(half * 16, 16), 16), :].astype(F32)
        mean = jnp.mean(values * values, axis=-1, keepdims=True)
        return (values * lax.rsqrt(mean + EPSILON) * gain[...].reshape(1, width)).astype(BF)

    mine[...] = normed(hold_l, g_l, core, DL)
    other[...] = normed(hold_l, g_l, 1 - core, DL)
    for at, half in ((0, core), (32, 1 - core)):
        value = normed(hold_s, g_s, half, DS)
        out_s[at : at + 16, :] = value[:, :KS]
        out_s[at + 16 : at + 32, :] = value[:, KS:]


def block_body(where, mine, other, across, got, small, out):
    out[0:16, :DL] = mine[...]
    out[16:32, :DL] = across[...]
    out[32:48, :DL] = other[...]
    out[48:64, :DL] = got[...]
    out[:, DL:] = small[...]


def project_body(
    where, near, z1, z2, z3, zf, s_got, w0, y1, y1_g, fo, fo_g, pr, y2, y2_g, fp, fp_g,
    order_l, order_s, kept_q, kept_kv, sent, kept_s, sent_s, rows_s,
):
    core, z, x = where[0], where[1], where[2]
    way = 2 * core - 1

    def at_z(step):
        return pl.ds(pl.multiple_of((z + 8 + step) % 8 * 16, 16), 16)

    def put(step, ref, row, col):
        rows_s[at_z(step), :KS] = ref[row : row + 16, col:]
        rows_s[at_z(step), KS:] = ref[row + 16 : row + 32, col:]

    put(0, near, 0, DL)
    put(4, zf, 0, DL)
    for i, ref in ((1, z1), (2, z2), (3, z3)):
        put(way * i, ref, 0, DL)
        put(-way * i, s_got, 32 * i - 32, 0)

    plain = ((w0, 0), (y1, 0), (fo, 0), (y1_g, 48), (w0, 48), (y1, 48), (fo_g, 0), (y1_g, 0))
    paired = ((pr, 0), (y2, 0), (fp, 0), (y2_g, 48), (pr, 48), (y2, 48), (fp_g, 0), (y2_g, 0))
    blocks = plain[:4] + paired[:4] + plain[4:] + paired[4:]
    total = None
    for k in range(0, DL, 512):
        at = slice(k, k + 512)
        cols = jnp.concatenate([ref[row : row + 48, at] for ref, row in blocks], 0)
        rows = jnp.concatenate([near[:32, at], z1[:, at], z2[:, at], z3[:, at], zf[:, at]], 0)
        term = dot_t(cols, rows)
        total = term if total is None else total + term
    total = total.astype(BF)

    def ordered(value, order):
        return lax.dot_general(
            value, order[...], (((0,), (0,)), ((), ())), preferred_element_type=F32
        ).astype(BF)

    own, other = total[:384, :], total[384:, :]
    mine = core == x % 2
    sent[...] = ordered(jnp.where(mine, other, own), order_l)
    value = ordered(jnp.where(mine, own, other), order_l)
    kept_q[...] = value[:, :HD]
    kept_kv[...] = value[:, HD:]

    small = None
    for q in range(3):
        cols = jnp.concatenate(
            [
                ref[row + 16 * q : row + 16 * q + 16, DL + PART * side : DL + PART * side + PART]
                for ref, row in paired
                for side in range(4)
            ],
            0,
        )
        term = dot_t(cols, rows_s[:, PART * q : PART * q + PART])
        small = term if small is None else small + term
    small = ordered(small.astype(BF), order_s)
    kept_s[...] = small[:, :256]
    sent_s[...] = small[:, 256:]


def attend(query, pairs, scores):
    top = None
    start = 0
    for ref, first, last in pairs:
        for lo in range(first, last, 512):
            count = 512
            block = dot_t(query, ref[lo : lo + count, :HD])
            scores[:, start : start + count] = block
            for at in range(0, count, 128):
                part = block[:, at : at + 128]
                top = part if top is None else jnp.maximum(top, part)
            start += count
    biggest = jnp.max(top, axis=1, keepdims=True)
    total, mixed = None, None
    start = 0
    for ref, first, last in pairs:
        for lo in range(first, last, 512):
            count = 512
            block = scores[:, start : start + count]
            weights = jnp.exp2((block - biggest) * (HD**-0.5 * LOG2E))
            for at in range(0, count, 128):
                part = weights[:, at : at + 128]
                total = part if total is None else total + part
            values = ref[lo : lo + count, HD:]
            term = jnp.dot(weights.astype(BF), values, preferred_element_type=F32)
            mixed = term if mixed is None else mixed + term
            start += count
    return (mixed / jnp.sum(total, axis=1, keepdims=True)).astype(BF)


def large_body(
    where, kept, taken, map_left, map_right, own, side, side_g, far, far_g,
    keep, send, scores, query,
):
    pairs = ((own, 0, 1024), (side, 0, 1024), (side_g, 0, 1024), (far, 0, 512), (far_g, 0, 512))
    core, z, x = where[0], where[1], where[2]
    way = 2 * core - 1
    keep[...] = jnp.zeros_like(keep)
    send[...] = jnp.zeros_like(send)
    query[:256, :] = kept[...]
    query[256:, :] = taken[:, :HD]

    @pl.loop(0, 2)
    def _(s):
        done = attend(query[pl.ds(pl.multiple_of(s * 256, 256), 256), :], pairs, scores)
        left = GUIDANCE * jnp.dot(done, map_left[...], preferred_element_type=F32)
        right = GUIDANCE * jnp.dot(done, map_right[...], preferred_element_type=F32)
        x_own = x ^ s

        def chip(step, x_at):
            return (z + 8 + step) % 8 * 4 + x_at

        def folded(row):
            return left[row : row + 8] + right[row + 8 : row + 16]

        for step, row in ((0, 0), (4, 224)) + tuple((way * i, 64 * i - 32) for i in (1, 2, 3)):
            keep[chip(step, x_own)] = folded(row)
            keep[chip(step, x_own ^ 3)] = folded(row + 16)
        for i in (1, 2, 3):
            send[chip(way * i, x_own)] = folded(64 * i)
            send[chip(way * i, x_own ^ 3)] = folded(64 * i + 16)


def pack_body(where, own, x1, x1_g, x2, got, x2_g, out):
    out[0:128, :] = own[...]
    out[128:256, :] = x1[0:128, :]
    out[256:384, :] = x1_g[128:256, :]
    out[384:512, :] = x2[...]
    out[512:640, :] = got[...]
    out[640:768, :] = x1[128:256, :]
    out[768:896, :] = x1_g[0:128, :]
    out[896:1024, :] = x2_g[...]


def small_body(
    where, query, map_left, map_right, keep, got, own, side, side_g, far, far_g, out, scores
):
    pairs = ((own, 0, 1024), (side, 0, 1024), (side_g, 0, 1024), (far, 0, 512), (far_g, 0, 512))
    x = where[2]
    done = attend(query[...], pairs, scores)
    left = (1.0 - GUIDANCE) * jnp.dot(done, map_left[...], preferred_element_type=F32)
    right = (1.0 - GUIDANCE) * jnp.dot(done, map_right[...], preferred_element_type=F32)
    out[...] = keep[...] + got[...]
    for z in range(8):
        out[z * 4 + x] += left[16 * z : 16 * z + 8] + right[16 * z + 8 : 16 * z + 16]


def shards(
    latent_large,
    latent_small,
    gain_large,
    gain_small,
    qkv_large,
    qkv_small,
    mix_large,
    mix_small,
    head_large,
    head_small,
):
    core, z, x, y = (lax.axis_index(name) for name in ("grp", "z", "x", "y"))
    x_low, z_low = x & 1, z & 1
    where = jnp.stack([core, z, x, y])

    mine, other, small = call(
        norm_body,
        [((16, DL), BF), ((16, DL), BF), ((64, KS), BF)],
        (where, latent_large, latent_small, gain_large, gain_small),
        [
            pltpu.VMEM((32, DL), BF),
            pltpu.VMEM((32, DS), BF),
            pltpu.VMEM((DL,), F32),
            pltpu.VMEM((DS,), F32),
            pltpu.SemaphoreType.DMA((4,)),
        ],
        limit=60,
        placed=[SMEM] + [ANY] * 4,
    )
    w, ws = qkv_large.T, qkv_small.T
    w_g = swap(w)
    xw = flip(w, "x", 1)
    across = cross(mine)
    w_g, ws, _ = tie(w_g, ws, mine)
    w0 = jnp.concatenate([w, w_g], 0)
    y1 = spread(w0, "y")
    ws = jnp.concatenate([ws, jnp.zeros((4, DS), BF)], 0)
    ws = jnp.concatenate([ws[:, :PART], ws[:, PART : 2 * PART], ws[:, 2 * PART :]], 0)
    ws_cross = cross(ws)
    (near,) = call(
        block_body, [((64, DL + KS), BF)], (where, mine, other, across, swap(across), small)
    )

    z1 = spread(near, "z")
    ws_cross, xw, _ = tie(ws_cross, xw, near)
    ws2 = jnp.concatenate([ws, ws_cross], 1)
    xw_g = swap(xw)
    ws4 = jnp.concatenate([ws2, flip(ws2, "x", 1)], 1)
    pr = jnp.concatenate(
        [jnp.concatenate([xw, ws4], 1), jnp.concatenate([xw_g, swap(ws4)], 1)], 0
    )
    y2 = spread(pr, "y")

    map_l = lax.dynamic_slice_in_dim(mix_large, (z * 2 + (x >> 1)) * HD, HD, 0)
    map_s = lax.dynamic_slice_in_dim(mix_small, (z >> 1) * HD, HD, 0)
    swapped = swap(jnp.concatenate([map_l, map_s], 0))
    map_l = jnp.where(core == x_low, map_l, swapped[:HD])
    map_s = jnp.where(core == z_low, map_s, swapped[HD:])
    blank = jnp.zeros((HD, 64), BF)
    maps = [
        jnp.concatenate(pair, 1)
        for pair in ((map_l, blank), (blank, map_l), (map_s, blank), (blank, map_s))
    ]

    def position(y_at):
        away = (y - y_at) & 3
        return jnp.where((away & 1 == 1) & (core == 1), 4 - away, away)

    source = lax.broadcasted_iota(jnp.int32, (384, 384), 0)
    target = lax.broadcasted_iota(jnp.int32, (384, 384), 1)
    block = target // 48
    from_l = jnp.where(block // 4 == x_low, 0, 4) + position(block & 3)
    order_l = (source == from_l * 48 + target % 48).astype(BF)
    source = lax.broadcasted_iota(jnp.int32, (512, 512), 0)
    target = lax.broadcasted_iota(jnp.int32, (512, 512), 1)
    group = jnp.where((target // 256 == 0) == (core == z_low), 0, 1)
    within = target % 256
    piece = within // 12
    mask = ((piece // 4) & 3) ^ x
    side = jnp.where(mask == 3, 1, jnp.where(mask == 1, 2, jnp.where(mask == 2, 3, 0)))
    from_s = (group * 16 + position(piece & 3) * 4 + side) * 16 + within % 12
    order_s = ((source == from_s) & (within < 192)).astype(BF)

    z1, order_l, order_s, *maps = tie(z1, order_l, order_s, *maps)
    z2 = spread(z1, "z")
    y1, _ = tie(y1, z1)
    fo = spread(y1[:48], "y")
    y1_g = swap(y1)

    z3 = spread(z2, "z")
    y2, fo, _ = tie(y2, fo, z2)
    fp = spread(y2[:48], "y")
    y2_g, fo_g = swap(y2), swap(fo)

    zf = spread(z3[:32], "z")
    s_got = swap(jnp.concatenate([v[32:, DL:] for v in (z1, z2, z3)], 0))
    fp, _ = tie(fp, z3)
    fp_g = swap(fp)

    kept_q, kept_kv, sent, kept_s, sent_s = call(
        project_body,
        [((256, HD), BF), ((256, 2 * HD), BF), ((256, 384), BF)] + [((128, 256), BF)] * 2,
        (
            where, near, z1, z2, z3, zf, s_got, w0, y1, y1_g, fo, fo_g, pr, y2, y2_g, fp, fp_g,
            order_l, order_s,
        ),
        [pltpu.VMEM((128, DS), BF)],
        limit=12,
    )

    taken, taken_s = tie(flip(sent, "x", 1), flip(sent_s, "z", 1))
    kept_g = swap(kept_kv)
    taken_g = swap(taken)
    all_l = jnp.concatenate([kept_kv, taken[:, HD:], kept_g, taken_g[:, HD:]], 0)
    k_side = spread(all_l, "y")

    kept_s, taken_s = kept_s[:, :192], taken_s[:, :192]
    head_s = jnp.where(
        z_low == 0,
        jnp.concatenate([kept_s, taken_s], 1),
        jnp.concatenate([taken_s, kept_s], 1),
    )
    own_s = head_s[:, HD:]
    got_s = swap(own_s)
    x1 = spread(jnp.concatenate([own_s, got_s], 0), "x")
    x2 = flip(own_s, "x", 2)
    x1_g, x2_g = swap(x1), swap(x2)
    (all_s,) = call(
        pack_body, [((1024, 2 * HD), BF)], (where, own_s, x1, x1_g, x2, got_s, x2_g)
    )
    s_side = spread(all_s, "y")
    k_side, _ = tie(k_side, all_s)
    k_far = spread(k_side[:512], "y")
    k_side_g = swap(k_side)
    k_far, s_side = tie(k_far, s_side)
    k_far_g = swap(k_far)
    s_far = spread(s_side[:512], "y")
    s_side_g = swap(s_side)

    keep, send = call(
        large_body,
        [((32, 8, 128), F32)] * 2,
        (where, kept_q, taken, *maps[:2], all_l, k_side, k_side_g, k_far, k_far_g),
        [pltpu.VMEM((256, 4096), F32), pltpu.VMEM((512, HD), BF)],
        flops=2**32,
    )
    keep, send, s_far = tie(keep, send, s_far)
    got = swap(send)
    s_far_g = swap(s_far)
    (total,) = call(
        small_body,
        [((32, 8, 128), F32)],
        (where, head_s[:, :HD], *maps[2:], keep, got, all_s, s_side, s_side_g, s_far, s_far_g),
        [pltpu.VMEM((128, 4096), F32)],
        flops=2**30,
    )

    returned = lax.all_to_all(total, ("z", "x"), split_axis=0, concat_axis=0, tiled=True)
    returned = jnp.sum(returned, axis=0)
    latent_l = lax.dynamic_slice_in_dim(latent_large, core * 16, 16, 0)
    latent_s = lax.dynamic_slice_in_dim(latent_small, core * 16, 16, 0)
    direct = GUIDANCE * jnp.dot(latent_l, head_large, preferred_element_type=F32) + (
        1.0 - GUIDANCE
    ) * jnp.dot(latent_s, head_small, preferred_element_type=F32)
    part = direct + jnp.concatenate([returned[:, :64], returned[:, 64:]], 0)
    other_part = swap(part)
    return jnp.where(
        core == 0,
        jnp.concatenate([part, other_part], 0),
        jnp.concatenate([other_part, part], 0),
    )


def solution(mesh):
    grid = Mesh(mesh.devices.reshape(2, 8, 4, 4), ("grp", "z", "x", "y"))
    tokens = ("z", "x", "y")
    return jax.shard_map(
        shards,
        mesh=grid,
        in_specs=(
            P(tokens, None),
            P(tokens, None),
            P(),
            P(),
            P(None, ("grp",) + tokens),
            P(None, ("grp",) + tokens),
            P("grp", None),
            P("grp", None),
            P(),
            P(),
        ),
        out_specs=P(tokens, None),
        check_vma=False,
    )
```

```python
import jax
import jax.numpy as jnp
from jax import lax
from jax.experimental import pallas as pl
from jax.experimental.pallas import tpu as pltpu
from jax.sharding import Mesh, PartitionSpec as P

HD = 128
GUIDANCE = 3.0
EPSILON = 1e-06
BF = jnp.bfloat16
F32 = jnp.float32
DL, DS = 5120, 1536
KS = DS // 2
PART = 512
LOG2E = 1.4426950408889634
VMEM = pl.BlockSpec(memory_space=pltpu.VMEM)
SMEM = pl.BlockSpec(memory_space=pltpu.SMEM)
ANY = pl.BlockSpec(memory_space=pl.ANY)
OPPOSITE = [(0, 3), (3, 0), (1, 2), (2, 1)]


def flip(block, axis, mask):
    count = lax.axis_size(axis)
    return lax.ppermute(block, axis, [(i, i ^ mask) for i in range(count)])


def swap(block):
    return flip(block, "grp", 1)


def cross(block):
    return lax.ppermute(block, "x", OPPOSITE)


def spread(block, axis):
    n = lax.axis_size(axis)
    pairs = [(i, (i + 1) % n) for i in range(n)]
    pairs += [(n + i, n + (i - 1) % n) for i in range(n)]
    return lax.ppermute(block, ("grp", axis), pairs)


def tie(*values):
    return lax.optimization_barrier(values)


def dot_t(rows, columns):
    return lax.dot_general(
        rows, columns, (((1,), (1,)), ((), ())), preferred_element_type=F32
    )


def call(body, outs, args, scratch=(), limit=16, placed=None, flops=0):
    return pl.pallas_call(
        body,
        out_shape=[jax.ShapeDtypeStruct(shape, dtype) for shape, dtype in outs],
        in_specs=placed or [SMEM] + [VMEM] * (len(args) - 1),
        out_specs=[VMEM] * len(outs),
        scratch_shapes=list(scratch),
        compiler_params=pltpu.CompilerParams(vmem_limit_bytes=limit * 2**20),
        cost_estimate=pl.CostEstimate(flops=flops, bytes_accessed=2**20, transcendentals=0),
    )(*args)


def pack(shape, pieces):
    def body(*refs):
        sources, out, sems = refs[: len(pieces)], refs[-2], refs[-1]
        tasks = []
        for i, (source, (_, part, to)) in enumerate(zip(sources, pieces)):
            source = source if part is None else source.at[part]
            tasks.append(pltpu.make_async_copy(source, out.at[to], sems.at[i]))
        for task in tasks:
            task.start()
        for task in tasks:
            task.wait()

    return pl.pallas_call(
        body,
        out_shape=jax.ShapeDtypeStruct(shape, BF),
        in_specs=[ANY] * len(pieces),
        out_specs=ANY,
        scratch_shapes=[pltpu.SemaphoreType.DMA((len(pieces),))],
        compiler_params=pltpu.CompilerParams(vmem_limit_bytes=2**20),
    )(*[piece[0] for piece in pieces])


def norm_body(
    where, large, small, gain_l, gain_s, mine, other, out_s, hold_l, hold_s, g_l, g_s, sems
):
    core = where[0]
    tasks = [
        pltpu.make_async_copy(source, target, sems.at[i])
        for i, (source, target) in enumerate(
            ((large, hold_l), (small, hold_s), (gain_l, g_l), (gain_s, g_s))
        )
    ]
    for task in tasks:
        task.start()
    for task in tasks:
        task.wait()

    def normed(latent, gain, half, width):
        values = latent[pl.ds(pl.multiple_of(half * 16, 16), 16), :].astype(F32)
        mean = jnp.mean(values * values, axis=-1, keepdims=True)
        return (values * lax.rsqrt(mean + EPSILON) * gain[...].reshape(1, width)).astype(BF)

    mine[...] = normed(hold_l, g_l, core, DL)
    other[...] = normed(hold_l, g_l, 1 - core, DL)
    for at, half in ((0, core), (32, 1 - core)):
        value = normed(hold_s, g_s, half, DS)
        out_s[at : at + 16, :] = value[:, :KS]
        out_s[at + 16 : at + 32, :] = value[:, KS:]


def ordered(value, order):
    return lax.dot_general(
        value, order[...], (((0,), (0,)), ((), ())), preferred_element_type=F32
    ).astype(BF)


def setup_body(where, mix_l, mix_s, order_l, order_s, maps):
    core, z, x, y = (where[i] for i in range(4))
    x_low, z_low = x % 2, z % 2

    def position(y_at):
        away = (y - y_at) & 3
        return jnp.where((away & 1 == 1) & (core == 1), 4 - away, away)

    def lines(size, axis):
        return lax.broadcasted_iota(jnp.int32, (1, size) if axis else (size, 1), axis)

    target = lines(384, 1)
    block = target // 48
    base = jnp.where(block // 4 == x_low, 0, 4) + position(block & 3)
    order_l[...] = (lines(384, 0) == base * 48 + target % 48).astype(F32).astype(BF)

    half = target // 192
    group = jnp.where((half == z_low) == (core == z_low), 0, 1)
    within = target % 192
    piece = within // 12
    mask = (piece // 4) ^ x
    side = jnp.where(mask == 3, 1, jnp.where(mask == 1, 2, jnp.where(mask == 2, 3, 0)))
    base = (group * 16 + position(piece & 3) * 4 + side) * 16 + within % 12
    order_s[...] = (lines(512, 0) == base).astype(F32).astype(BF)

    maps[:64, :] = mix_l[:, pl.ds(pl.multiple_of((z * 2 + x // 2) * HD, HD), HD)]
    maps[64:, :] = mix_s[:, pl.ds(pl.multiple_of(z // 2 * HD, HD), HD)]


def sides(mine, own, other):
    rows = jnp.where(mine, own, other)
    blank = jnp.zeros_like(rows)
    return jnp.concatenate([rows, blank], 0), jnp.concatenate([blank, rows], 0)


def project_small_body(
    where, own, s1, a1, a2, a3, got, ws, ws_g, yz, yz_g, far, far_g, order, query, pairs, rows
):
    core, z = where[0], where[1]
    way = 2 * core - 1

    def put(step, ref, row, col):
        at = pl.ds(pl.multiple_of((z + 8 + step) % 8 * 16, 16), 16)
        rows[at, :KS] = ref[row : row + 16, col:]
        rows[at, KS:] = ref[row + 16 : row + 32, col:]

    put(0, own, 0, 0)
    put(4, a3, 0, DL)
    for i, ref, col in ((1, s1, 0), (2, a1, DL), (3, a2, DL)):
        put(way * i, ref, 0, col)
        put(-way * i, got, 32 * i - 32, 0)

    blocks = (
        (ws, 0), (yz, 2 * DL), (far, 0), (yz_g, 2 * DL + 4 * PART),
        (ws_g, 0), (yz, 2 * DL + 4 * PART), (far_g, 0), (yz_g, 2 * DL),
    )
    small = None
    for q in range(3):
        cols = jnp.concatenate(
            [
                ref[16 * q : 16 * q + 16, col + PART * side : col + PART * side + PART]
                for ref, col in blocks
                for side in range(4)
            ],
            0,
        )
        term = dot_t(cols, rows[:, PART * q : PART * q + PART])
        small = term if small is None else small + term
    small = ordered(small.astype(BF), order)
    query[...] = small[:, :HD]
    pairs[...] = small[:, HD:]


def project_body(
    where, near, a1, a2, a3, a4, b1, b2, b3, w0, y1, y1_g, pr, y2, y2_g, far, far_g,
    order, kept, sent,
):
    core, x = where[0], where[2]
    blocks = (
        (w0, 0, 0), (y1, 0, 0), (far, 0, 0), (y1_g, 48, 0),
        (pr, 0, 0), (y2, 0, 0), (far, 0, DL), (y2_g, 48, 0),
        (w0, 48, 0), (y1, 48, 0), (far_g, 0, 0), (y1_g, 0, 0),
        (pr, 48, 0), (y2, 48, 0), (far_g, 0, DL), (y2_g, 0, 0),
    )
    total = None
    for k in range(0, DL, 1024):
        at = slice(k, k + 1024)
        cols = jnp.concatenate(
            [ref[row : row + 48, col + k : col + k + 1024] for ref, row, col in blocks], 0
        )
        rows = jnp.concatenate([ref[:, at] for ref in (near, a1, b1, a2, b2, a3, b3, a4)], 0)
        term = dot_t(cols, rows)
        total = term if total is None else total + term
    total = total.astype(BF)
    own, other = total[:384, :], total[384:, :]
    mine = core == x % 2
    sent[...] = ordered(jnp.where(mine, other, own), order)
    kept[...] = ordered(jnp.where(mine, own, other), order)


def attend(query, pairs, scores):
    top = None
    start = 0
    for ref, first, last in pairs:
        for lo in range(first, last, 512):
            count = 512
            block = dot_t(query, ref[lo : lo + count, :HD])
            scores[:, start : start + count] = block
            for at in range(0, count, 128):
                part = block[:, at : at + 128]
                top = part if top is None else jnp.maximum(top, part)
            start += count
    biggest = jnp.max(top, axis=1, keepdims=True)
    total, mixed = None, None
    start = 0
    for ref, first, last in pairs:
        for lo in range(first, last, 512):
            count = 512
            block = scores[:, start : start + count]
            weights = jnp.exp2((block - biggest) * (HD**-0.5 * LOG2E))
            for at in range(0, count, 128):
                part = weights[:, at : at + 128]
                total = part if total is None else total + part
            values = ref[lo : lo + count, HD:]
            term = jnp.dot(weights.astype(BF), values, preferred_element_type=F32)
            mixed = term if mixed is None else mixed + term
            start += count
    return (mixed / jnp.sum(total, axis=1, keepdims=True)).astype(BF)


def large_body(
    where, kept, taken, maps, maps_g, own, side, side_g, far, far_g,
    keep, send, scores, query,
):
    pairs = ((own, 0, 1024), (side, 0, 1024), (side_g, 0, 1024), (far, 0, 512), (far_g, 0, 512))
    core, z, x = where[0], where[1], where[2]
    way = 2 * core - 1
    keep[...] = jnp.zeros_like(keep)
    send[...] = jnp.zeros_like(send)
    query[:256, :] = kept[:, :HD]
    query[256:, :] = taken[:, :HD]
    map_left, map_right = sides(core == x % 2, maps[:64, :], maps_g[:64, :])

    @pl.loop(0, 2)
    def _(s):
        done = attend(query[pl.ds(pl.multiple_of(s * 256, 256), 256), :], pairs, scores)
        left = GUIDANCE * dot_t(done, map_left)
        right = GUIDANCE * dot_t(done, map_right)
        x_own = x ^ s

        def chip(step, x_at):
            return (z + 8 + step) % 8 * 4 + x_at

        def folded(row):
            return left[row : row + 8] + right[row + 8 : row + 16]

        for step, row in ((0, 0), (4, 224)) + tuple((way * i, 64 * i - 32) for i in (1, 2, 3)):
            keep[chip(step, x_own)] = folded(row)
            keep[chip(step, x_own ^ 3)] = folded(row + 16)
        for i in (1, 2, 3):
            send[chip(way * i, x_own)] = folded(64 * i)
            send[chip(way * i, x_own ^ 3)] = folded(64 * i + 16)


def small_body(
    where, query, maps, maps_g, keep, got, own, side, side_g, far, far_g, out, scores
):
    pairs = ((own, 0, 1024), (side, 0, 1024), (side_g, 0, 1024), (far, 0, 512), (far_g, 0, 512))
    core, z_at, x = where[0], where[1], where[2]
    map_left, map_right = sides(core == z_at % 2, maps[64:, :], maps_g[64:, :])
    done = attend(query[...], pairs, scores)
    left = (1.0 - GUIDANCE) * dot_t(done, map_left)
    right = (1.0 - GUIDANCE) * dot_t(done, map_right)
    out[...] = keep[...] + got[...]
    for z in range(8):
        out[z * 4 + x] += left[16 * z : 16 * z + 8] + right[16 * z + 8 : 16 * z + 16]


def shards(
    latent_large,
    latent_small,
    gain_large,
    gain_small,
    qkv_large,
    qkv_small,
    mix_large,
    mix_small,
    head_large,
    head_small,
):
    core, z, x, y = (lax.axis_index(name) for name in ("grp", "z", "x", "y"))
    x_low, z_low = x & 1, z & 1
    where = jnp.stack([core, z, x, y])

    mine, other, s0 = call(
        norm_body,
        [((16, DL), BF), ((16, DL), BF), ((64, KS), BF)],
        (where, latent_large, latent_small, gain_large, gain_small),
        [
            pltpu.VMEM((32, DL), BF),
            pltpu.VMEM((32, DS), BF),
            pltpu.VMEM((DL,), F32),
            pltpu.VMEM((DS,), F32),
            pltpu.SemaphoreType.DMA((4,)),
        ],
        limit=60,
        placed=[SMEM] + [ANY] * 4,
    )
    w, ws = qkv_large.T, qkv_small.T
    w_g = swap(w)
    xw = flip(w, "x", 1)
    across = cross(mine)
    s1 = spread(s0, "z")
    ws, mix_l, mix_s, _ = tie(ws, mix_large.T, mix_small.T, mine)
    top, low, left, right = slice(0, 48), slice(48, 96), slice(0, DL), slice(DL, None)
    near, pair, every = slice(0, 16), slice(16, 32), slice(None)
    order_l, order_s, maps = call(
        setup_body,
        [((384, 384), BF), ((512, 384), BF), ((HD, HD), BF)],
        (where, mix_l, mix_s),
    )
    w_g, _ = tie(w_g, mine)
    w0 = pack((96, DL), [(w, None, top), (w_g, None, low)])
    y1 = spread(w0, "y")
    ws = jnp.concatenate([ws, jnp.zeros((4, DS), BF)], 0)
    ws = jnp.concatenate([ws[:, :PART], ws[:, PART : 2 * PART], ws[:, 2 * PART :]], 0)
    trade = [(g * 8 + i, (1 - g) * 8 + (i ^ 1)) for g in range(2) for i in range(8) if i % 2 != g]
    ws_other = lax.ppermute(ws, ("grp", "z"), trade)

    across, s1, w0, ws_other = tie(across, s1, w0, ws_other)
    ws = jnp.where(core == z_low, ws, ws_other)
    ws_cross = cross(ws)

    def block(own, facing, small):
        return pack(
            (32, DL + KS),
            [
                (own, None, (near, left)),
                (facing, None, (pair, left)),
                (s1, small, (every, right)),
            ],
        )

    a0 = block(mine, across, slice(0, 32))
    a1 = spread(a0, "z")
    across, xw, _ = tie(across, xw, a0)
    b0 = block(other, swap(across), slice(32, 64))
    pr = pack((96, DL), [(xw, None, top), (swap(xw), None, low)])

    a1, b0, y1, pr, ws_cross, maps = tie(a1, b0, y1, pr, ws_cross, maps)
    a2 = spread(a1, "z")
    b1 = spread(b0, "z")
    y2 = spread(pr, "y")
    ws2 = jnp.concatenate([ws, ws_cross], 1)
    ws4 = jnp.concatenate([ws2, flip(ws2, "x", 1)], 1)
    ws4_g = swap(ws4)
    y1_g = swap(y1)
    maps_g = swap(maps)

    a2, b1, y1, y1_g, y2, ws4, ws4_g, maps_g = tie(a2, b1, y1, y1_g, y2, ws4, ws4_g, maps_g)
    a3 = spread(a2, "z")
    b2 = spread(b1, "z")
    ends = [slice(DL, 2 * DL), slice(2 * DL, 2 * DL + 4 * PART), slice(2 * DL + 4 * PART, None)]
    yz = spread(
        pack(
            (48, 2 * DL + 8 * PART),
            [(y1, top, (every, left)), (y2, top, (every, ends[0]))]
            + [(ws4, None, (every, ends[1])), (ws4_g, None, (every, ends[2]))],
        ),
        "y",
    )
    y2_g = swap(y2)

    a3, b2, y2_g = tie(a3, b2, y2_g)
    a4 = spread(a3, "z")
    b3 = spread(b2, "z")
    s_got = swap(
        pack(
            (96, KS),
            [
                (s1, slice(32, 64), slice(0, 32)),
                (b1, (every, right), slice(32, 64)),
                (b2, (every, right), slice(64, 96)),
            ],
        )
    )

    a4, b3, yz, s_got = tie(a4, b3, yz, s_got)
    far_s = spread(pack((48, 4 * PART), [(yz, (every, ends[1]), every)]), "y")
    yz_g = swap(yz)
    kept, sent = call(
        project_body,
        [((256, 384), BF)] * 2,
        (where, a0, a1, a2, a3, a4, b1, b2, b3)
        + (w0, y1, y1_g, pr, y2, y2_g, yz, yz_g, order_l),
        limit=12,
        flops=2**32,
    )

    taken = flip(sent, "x", 1)
    kept_g = swap(kept)
    far_s, _ = tie(far_s, sent)
    far_s_g = swap(far_s)
    query_s, own_s = call(
        project_small_body,
        [((128, HD), BF), ((128, 2 * HD), BF)],
        (where, s0, s1, a1, a2, a3, s_got, ws4, ws4_g, yz, yz_g, far_s, far_s_g, order_s),
        [pltpu.VMEM((128, DS), BF)],
        limit=6,
        flops=2**29,
    )
    got_s = swap(own_s)
    taken, got_s = tie(taken, got_s)
    x1 = spread(jnp.concatenate([own_s, got_s], 0), "x")
    x2 = flip(own_s, "x", 2)

    pairs = slice(HD, None)
    taken_g = swap(taken)
    all_l = pack(
        (1024, 2 * HD),
        [
            (value, (every, pairs), slice(256 * i, 256 * i + 256))
            for i, value in enumerate((kept, taken, kept_g, taken_g))
        ],
    )
    k_side = spread(all_l, "y")

    x1_g, x2_g = swap(x1), swap(x2)
    first, second = slice(0, 128), slice(128, 256)
    parts = ((own_s, None), (x1, first), (x1_g, second), (x2, None))
    parts += ((got_s, None), (x1, second), (x1_g, first), (x2_g, None))
    all_s = pack(
        (1024, 2 * HD),
        [(value, part, slice(128 * i, 128 * i + 128)) for i, (value, part) in enumerate(parts)],
    )
    s_side = spread(all_s, "y")
    k_side, _ = tie(k_side, all_s)
    k_far = spread(k_side[:512], "y")
    k_side_g = swap(k_side)
    k_far, _ = tie(k_far, s_side)
    k_far_g = swap(k_far)
    s_far = spread(s_side[:512], "y")
    s_side_g = swap(s_side)

    keep, send = call(
        large_body,
        [((32, 8, 128), F32)] * 2,
        (where, kept, taken, maps, maps_g, all_l, k_side, k_side_g, k_far, k_far_g),
        [pltpu.VMEM((256, 4096), F32), pltpu.VMEM((512, HD), BF)],
        flops=2**32,
    )
    keep, send, s_far = tie(keep, send, s_far)
    got = swap(send)
    s_far_g = swap(s_far)
    (total,) = call(
        small_body,
        [((32, 8, 128), F32)],
        (where, query_s, maps, maps_g, keep, got, all_s, s_side, s_side_g, s_far, s_far_g),
        [pltpu.VMEM((128, 4096), F32)],
        flops=2**30,
    )

    returned = lax.all_to_all(total, ("z", "x"), split_axis=0, concat_axis=0, tiled=True)
    returned = jnp.sum(returned, axis=0)
    latent_l = lax.dynamic_slice_in_dim(latent_large, core * 16, 16, 0)
    latent_s = lax.dynamic_slice_in_dim(latent_small, core * 16, 16, 0)
    direct = GUIDANCE * jnp.dot(latent_l, head_large, preferred_element_type=F32) + (
        1.0 - GUIDANCE
    ) * jnp.dot(latent_s, head_small, preferred_element_type=F32)
    part = direct + jnp.concatenate([returned[:, :64], returned[:, 64:]], 0)
    other_part = swap(part)
    return jnp.where(
        core == 0,
        jnp.concatenate([part, other_part], 0),
        jnp.concatenate([other_part, part], 0),
    )


def solution(mesh):
    grid = Mesh(mesh.devices.reshape(2, 8, 4, 4), ("grp", "z", "x", "y"))
    tokens = ("z", "x", "y")
    return jax.shard_map(
        shards,
        mesh=grid,
        in_specs=(
            P(tokens, None),
            P(tokens, None),
            P(),
            P(),
            P(None, ("grp",) + tokens),
            P(None, ("grp",) + tokens),
            P("grp", None),
            P("grp", None),
            P(),
            P(),
        ),
        out_specs=P(tokens, None),
        check_vma=False,
    )
```

```python
import jax
import jax.numpy as jnp
from jax import lax
from jax.experimental import pallas as pl
from jax.experimental.pallas import tpu as pltpu
from jax.sharding import Mesh, PartitionSpec as P

HD = 128
GUIDANCE = 3.0
EPSILON = 1e-06
BF = jnp.bfloat16
F32 = jnp.float32
DL, DS = 5120, 1536
KS = DS // 2
PART = 512
LOG2E = 1.4426950408889634
VMEM = pl.BlockSpec(memory_space=pltpu.VMEM)
SMEM = pl.BlockSpec(memory_space=pltpu.SMEM)
ANY = pl.BlockSpec(memory_space=pl.ANY)
OPPOSITE = [(0, 3), (3, 0), (1, 2), (2, 1)]


def flip(block, axis, mask):
    count = lax.axis_size(axis)
    return lax.ppermute(block, axis, [(i, i ^ mask) for i in range(count)])


def swap(block):
    return flip(block, "grp", 1)


def cross(block):
    return lax.ppermute(block, "x", OPPOSITE)


def spread(block, axis):
    n = lax.axis_size(axis)
    pairs = [(i, (i + 1) % n) for i in range(n)]
    pairs += [(n + i, n + (i - 1) % n) for i in range(n)]
    return lax.ppermute(block, ("grp", axis), pairs)


def tie(*values):
    return lax.optimization_barrier(values)


def dot_t(rows, columns):
    return lax.dot_general(
        rows, columns, (((1,), (1,)), ((), ())), preferred_element_type=F32
    )


def call(body, outs, args, scratch=(), limit=16, placed=None, flops=0):
    return pl.pallas_call(
        body,
        out_shape=[jax.ShapeDtypeStruct(shape, dtype) for shape, dtype in outs],
        in_specs=placed or [SMEM] + [VMEM] * (len(args) - 1),
        out_specs=[VMEM] * len(outs),
        scratch_shapes=list(scratch),
        compiler_params=pltpu.CompilerParams(vmem_limit_bytes=limit * 2**20),
        cost_estimate=pl.CostEstimate(flops=flops, bytes_accessed=2**20, transcendentals=0),
    )(*args)


def pack(shape, pieces):
    def body(*refs):
        sources, out, sems = refs[: len(pieces)], refs[-2], refs[-1]
        tasks = []
        for i, (source, (_, part, to)) in enumerate(zip(sources, pieces)):
            source = source if part is None else source.at[part]
            tasks.append(pltpu.make_async_copy(source, out.at[to], sems.at[i]))
        for task in tasks:
            task.start()
        for task in tasks:
            task.wait()

    return pl.pallas_call(
        body,
        out_shape=jax.ShapeDtypeStruct(shape, BF),
        in_specs=[ANY] * len(pieces),
        out_specs=ANY,
        scratch_shapes=[pltpu.SemaphoreType.DMA((len(pieces),))],
        compiler_params=pltpu.CompilerParams(vmem_limit_bytes=2**20),
    )(*[piece[0] for piece in pieces])


def norm_body(
    where, large, small, gain_l, gain_s, mine, other, out_s, hold_l, hold_s, g_l, g_s, sems
):
    core = where[0]
    tasks = [
        pltpu.make_async_copy(source, target, sems.at[i])
        for i, (source, target) in enumerate(
            ((large, hold_l), (small, hold_s), (gain_l, g_l), (gain_s, g_s))
        )
    ]
    for task in tasks:
        task.start()
    for task in tasks:
        task.wait()

    def normed(latent, gain, half, width):
        values = latent[pl.ds(pl.multiple_of(half * 16, 16), 16), :].astype(F32)
        mean = jnp.mean(values * values, axis=-1, keepdims=True)
        return (values * lax.rsqrt(mean + EPSILON) * gain[...].reshape(1, width)).astype(BF)

    mine[...] = normed(hold_l, g_l, core, DL)
    other[...] = normed(hold_l, g_l, 1 - core, DL)
    for at, half in ((0, core), (32, 1 - core)):
        value = normed(hold_s, g_s, half, DS)
        out_s[at : at + 16, :] = value[:, :KS]
        out_s[at + 16 : at + 32, :] = value[:, KS:]


def ordered(value, order):
    return lax.dot_general(
        value, order[...], (((0,), (0,)), ((), ())), preferred_element_type=F32
    ).astype(BF)


def setup_body(where, mix_l, mix_s, order_l, order_s, maps):
    core, z, x, y = (where[i] for i in range(4))
    x_low, z_low = x % 2, z % 2

    def position(y_at):
        away = (y - y_at) & 3
        return jnp.where((away & 1 == 1) & (core == 1), 4 - away, away)

    def lines(size, axis):
        return lax.broadcasted_iota(jnp.int32, (1, size) if axis else (size, 1), axis)

    target = lines(384, 1)
    block = target // 48
    base = jnp.where(block // 4 == x_low, 0, 4) + position(block & 3)
    order_l[...] = (lines(384, 0) == base * 48 + target % 48).astype(F32).astype(BF)

    half = target // 192
    group = jnp.where((half == z_low) == (core == z_low), 0, 1)
    within = target % 192
    piece = within // 12
    mask = (piece // 4) ^ x
    side = jnp.where(mask == 3, 1, jnp.where(mask == 1, 2, jnp.where(mask == 2, 3, 0)))
    base = (group * 16 + position(piece & 3) * 4 + side) * 16 + within % 12
    order_s[...] = (lines(512, 0) == base).astype(F32).astype(BF)

    maps[:64, :] = mix_l[:, pl.ds(pl.multiple_of((z * 2 + x // 2) * HD, HD), HD)]
    maps[64:, :] = mix_s[:, pl.ds(pl.multiple_of(z // 2 * HD, HD), HD)]


def sides(mine, own, other):
    rows = jnp.where(mine, own, other)
    blank = jnp.zeros_like(rows)
    return jnp.concatenate([rows, blank], 0), jnp.concatenate([blank, rows], 0)


def project_small_body(
    where, own, s1, z1, z2, z3, got, ws, ws_g, yz, yz_g, far, far_g, order, query, pairs, rows
):
    core, z = where[0], where[1]
    way = 2 * core - 1

    def put(step, ref, row, col):
        at = pl.ds(pl.multiple_of((z + 8 + step) % 8 * 16, 16), 16)
        rows[at, :KS] = ref[row : row + 16, col:]
        rows[at, KS:] = ref[row + 16 : row + 32, col:]

    put(0, own, 0, 0)
    put(4, z3, 0, DL)
    for i, ref, col in ((1, s1, 0), (2, z1, DL), (3, z2, DL)):
        put(way * i, ref, 0, col)
        put(-way * i, got, 32 * i - 32, 0)

    blocks = (
        (ws, 0), (yz, 2 * DL), (far, 0), (yz_g, 2 * DL + 4 * PART),
        (ws_g, 0), (yz, 2 * DL + 4 * PART), (far_g, 0), (yz_g, 2 * DL),
    )
    small = None
    for q in range(3):
        cols = jnp.concatenate(
            [
                ref[16 * q : 16 * q + 16, col + PART * side : col + PART * side + PART]
                for ref, col in blocks
                for side in range(4)
            ],
            0,
        )
        term = dot_t(cols, rows[:, PART * q : PART * q + PART])
        small = term if small is None else small + term
    small = ordered(small.astype(BF), order)
    query[...] = small[:, :HD]
    pairs[...] = small[:, HD:]


def project_body(
    where, near, z1, z2, z3, z4, w0, y1, y1_g, yz, pr, y2, y2_g, own, other
):
    blocks = (
        (w0, 0, 0), (y1, 0, 0), (yz, 0, 0), (y1_g, 48, 0),
        (pr, 0, 0), (y2, 0, 0), (yz, 0, DL), (y2_g, 48, 0),
        (w0, 48, 0), (y1, 48, 0), (y1_g, 0, 0), (pr, 48, 0), (y2, 48, 0), (y2_g, 0, 0),
    )
    total = product(blocks, (near, z1, z2, z3, z4))
    own[...] = total[:384, :]
    other[...] = total[384:, :]


def product(blocks, rows):
    near, z1, z2, z3, z4 = rows
    total = None
    for k in range(0, DL, 1024):
        at = slice(k, k + 1024)
        cols = jnp.concatenate(
            [ref[row : row + 48, col + k : col + k + 1024] for ref, row, col in blocks], 0
        )
        parts = [near[:, at], z1[:, at], z2[32:, at], z2[:32, at], z3[32:, at]]
        parts += [z3[:32, at], z4[32:, at], z4[:32, at]]
        term = dot_t(cols, jnp.concatenate(parts, 0))
        total = term if total is None else total + term
    return total.astype(BF)


def finish_body(where, near, z1, z2, z3, z4, yz_g, own, other, order, kept, sent):
    core, x = where[0], where[2]
    far = product(((yz_g, 0, 0), (yz_g, 0, DL)), (near, z1, z2, z3, z4))
    parts = [other[0:96, :], far[:48, :], other[96:240, :], far[48:, :], other[240:, :]]
    first, second = own[...], jnp.concatenate(parts, 0)
    mine = core == x % 2
    sent[...] = ordered(jnp.where(mine, second, first), order)
    kept[...] = ordered(jnp.where(mine, first, second), order)


def attend(query, pairs, scores):
    top = None
    start = 0
    for ref, first, last in pairs:
        for lo in range(first, last, 512):
            count = 512
            block = dot_t(query, ref[lo : lo + count, :HD])
            scores[:, start : start + count] = block
            for at in range(0, count, 128):
                part = block[:, at : at + 128]
                top = part if top is None else jnp.maximum(top, part)
            start += count
    biggest = jnp.max(top, axis=1, keepdims=True)
    total, mixed = None, None
    start = 0
    for ref, first, last in pairs:
        for lo in range(first, last, 512):
            count = 512
            block = scores[:, start : start + count]
            weights = jnp.exp2((block - biggest) * (HD**-0.5 * LOG2E))
            for at in range(0, count, 128):
                part = weights[:, at : at + 128]
                total = part if total is None else total + part
            values = ref[lo : lo + count, HD:]
            term = jnp.dot(weights.astype(BF), values, preferred_element_type=F32)
            mixed = term if mixed is None else mixed + term
            start += count
    return (mixed / jnp.sum(total, axis=1, keepdims=True)).astype(BF)


def large_body(
    where, kept, taken, maps, maps_g, own, side, side_g, far, far_g,
    keep, send, scores, query,
):
    pairs = ((own, 0, 1024), (side, 0, 1024), (side_g, 0, 1024), (far, 0, 512), (far_g, 0, 512))
    core, z, x = where[0], where[1], where[2]
    way = 2 * core - 1
    keep[...] = jnp.zeros_like(keep)
    send[...] = jnp.zeros_like(send)
    query[:256, :] = kept[:, :HD]
    query[256:, :] = taken[:, :HD]
    map_left, map_right = sides(core == x % 2, maps[:64, :], maps_g[:64, :])

    @pl.loop(0, 2)
    def _(s):
        done = attend(query[pl.ds(pl.multiple_of(s * 256, 256), 256), :], pairs, scores)
        left = GUIDANCE * dot_t(done, map_left)
        right = GUIDANCE * dot_t(done, map_right)
        x_own = x ^ s

        def chip(step, x_at):
            return (z + 8 + step) % 8 * 4 + x_at

        def folded(row):
            return left[row : row + 8] + right[row + 8 : row + 16]

        for step, row in ((0, 0), (4, 224)) + tuple((way * i, 64 * i - 32) for i in (1, 2, 3)):
            keep[chip(step, x_own)] = folded(row)
            keep[chip(step, x_own ^ 3)] = folded(row + 16)
        for i in (1, 2, 3):
            send[chip(way * i, x_own)] = folded(64 * i)
            send[chip(way * i, x_own ^ 3)] = folded(64 * i + 16)


def small_body(
    where, query, maps, maps_g, keep, got, own, side, side_g, far, far_g, out, scores
):
    pairs = ((own, 0, 1024), (side, 0, 1024), (side_g, 0, 1024), (far, 0, 512), (far_g, 0, 512))
    core, z_at, x = where[0], where[1], where[2]
    map_left, map_right = sides(core == z_at % 2, maps[64:, :], maps_g[64:, :])
    done = attend(query[...], pairs, scores)
    left = (1.0 - GUIDANCE) * dot_t(done, map_left)
    right = (1.0 - GUIDANCE) * dot_t(done, map_right)
    out[...] = keep[...] + got[...]
    for z in range(8):
        out[z * 4 + x] += left[16 * z : 16 * z + 8] + right[16 * z + 8 : 16 * z + 16]


def shards(
    latent_large,
    latent_small,
    gain_large,
    gain_small,
    qkv_large,
    qkv_small,
    mix_large,
    mix_small,
    head_large,
    head_small,
):
    core, z, x, y = (lax.axis_index(name) for name in ("grp", "z", "x", "y"))
    x_low, z_low = x & 1, z & 1
    where = jnp.stack([core, z, x, y])

    mine, other, s0 = call(
        norm_body,
        [((16, DL), BF), ((16, DL), BF), ((64, KS), BF)],
        (where, latent_large, latent_small, gain_large, gain_small),
        [
            pltpu.VMEM((32, DL), BF),
            pltpu.VMEM((32, DS), BF),
            pltpu.VMEM((DL,), F32),
            pltpu.VMEM((DS,), F32),
            pltpu.SemaphoreType.DMA((4,)),
        ],
        limit=60,
        placed=[SMEM] + [ANY] * 4,
    )
    w, ws = qkv_large.T, qkv_small.T
    w_g = swap(w)
    xw = flip(w, "x", 1)
    across = cross(mine)
    s1 = spread(s0, "z")
    w_g, ws, mix_l, mix_s, _ = tie(w_g, ws, mix_large.T, mix_small.T, mine)
    top, low, left, right = slice(0, 48), slice(48, 96), slice(0, DL), slice(DL, None)
    near, pair, every = slice(0, 16), slice(16, 32), slice(None)
    ws = jnp.concatenate([ws, jnp.zeros((4, DS), BF)], 0)
    ws = jnp.concatenate([ws[:, :PART], ws[:, PART : 2 * PART], ws[:, 2 * PART :]], 0)
    trade = [(g * 8 + i, (1 - g) * 8 + (i ^ 1)) for g in range(2) for i in range(8) if i % 2 != g]
    ws_other = lax.ppermute(ws, ("grp", "z"), trade)
    w0 = pack((96, DL), [(w, None, top), (w_g, None, low)])
    y1 = spread(w0, "y")
    order_l, order_s, maps = call(
        setup_body,
        [((384, 384), BF), ((512, 384), BF), ((HD, HD), BF)],
        (where, mix_l, mix_s),
    )

    across, s1, w0, ws_other = tie(across, s1, w0, ws_other)
    ws = jnp.where(core == z_low, ws, ws_other)
    ws_cross = cross(ws)

    def block(at, own, facing, small):
        return [
            (own, None, (slice(at, at + 16), left)),
            (facing, None, (slice(at + 16, at + 32), left)),
            (s1, small, (slice(at, at + 32), right)),
        ]

    a0 = pack((32, DL + KS), block(0, mine, across, slice(0, 32)))
    z1 = spread(a0, "z")
    across, xw, _ = tie(across, xw, a0)
    got = swap(across)
    pr = pack((96, DL), [(xw, None, top), (swap(xw), None, low)])

    z1, y1, got, pr, ws_cross, maps = tie(z1, y1, got, pr, ws_cross, maps)
    z2 = spread(
        pack((64, DL + KS), [(z1, None, slice(0, 32))] + block(32, other, got, slice(32, 64))), "z"
    )
    y2 = spread(pr, "y")
    ws2 = jnp.concatenate([ws, ws_cross], 1)
    ws4 = jnp.concatenate([ws2, flip(ws2, "x", 1)], 1)
    ws4_g = swap(ws4)
    y1_g = swap(y1)
    maps_g = swap(maps)

    z2, y1, y1_g, y2, ws4, ws4_g, maps_g = tie(z2, y1, y1_g, y2, ws4, ws4_g, maps_g)
    z3 = spread(z2, "z")
    ends = [slice(DL, 2 * DL), slice(2 * DL, 2 * DL + 4 * PART), slice(2 * DL + 4 * PART, None)]
    yz = spread(
        pack(
            (48, 2 * DL + 8 * PART),
            [(y1, top, (every, left)), (y2, top, (every, ends[0]))]
            + [(ws4, None, (every, ends[1])), (ws4_g, None, (every, ends[2]))],
        ),
        "y",
    )
    y2_g = swap(y2)

    z3, y2_g = tie(z3, y2_g)
    z4 = spread(z3, "z")
    s_got = swap(
        pack(
            (96, KS),
            [
                (s1, slice(32, 64), slice(0, 32)),
                (z2, (slice(32, 64), right), slice(32, 64)),
                (z3, (slice(32, 64), right), slice(64, 96)),
            ],
        )
    )

    z4, yz, s_got = tie(z4, yz, s_got)
    far_s = spread(pack((48, 4 * PART), [(yz, (every, ends[1]), every)]), "y")
    yz_g = swap(yz)
    own, another = call(
        project_body,
        [((384, 256), BF), ((288, 256), BF)],
        (where, a0, z1, z2, z3, z4, w0, y1, y1_g, yz, pr, y2, y2_g),
        limit=12,
        flops=2**32,
    )
    kept, sent = call(
        finish_body,
        [((256, 384), BF)] * 2,
        (where, a0, z1, z2, z3, z4, yz_g, own, another, order_l),
        limit=12,
        flops=2**29,
    )

    taken = flip(sent, "x", 1)
    kept_g = swap(kept)
    far_s, _ = tie(far_s, sent)
    far_s_g = swap(far_s)
    query_s, own_s = call(
        project_small_body,
        [((128, HD), BF), ((128, 2 * HD), BF)],
        (where, s0, s1, z1, z2, z3, s_got, ws4, ws4_g, yz, yz_g, far_s, far_s_g, order_s),
        [pltpu.VMEM((128, DS), BF)],
        limit=6,
        flops=2**29,
    )
    got_s = swap(own_s)
    taken, got_s = tie(taken, got_s)
    x1 = spread(jnp.concatenate([own_s, got_s], 0), "x")
    x2 = flip(own_s, "x", 2)

    pairs = slice(HD, None)
    taken_g = swap(taken)
    all_l = pack(
        (1024, 2 * HD),
        [
            (value, (every, pairs), slice(256 * i, 256 * i + 256))
            for i, value in enumerate((kept, taken, kept_g, taken_g))
        ],
    )
    k_side = spread(all_l, "y")

    x1_g, x2_g = swap(x1), swap(x2)
    first, second = slice(0, 128), slice(128, 256)
    parts = ((own_s, None), (x1, first), (x1_g, second), (x2, None))
    parts += ((got_s, None), (x1, second), (x1_g, first), (x2_g, None))
    all_s = pack(
        (1024, 2 * HD),
        [(value, part, slice(128 * i, 128 * i + 128)) for i, (value, part) in enumerate(parts)],
    )
    s_side = spread(all_s, "y")
    k_side, _ = tie(k_side, all_s)
    k_far = spread(k_side[:512], "y")
    k_side_g = swap(k_side)
    k_far, _ = tie(k_far, s_side)
    k_far_g = swap(k_far)
    s_far = spread(s_side[:512], "y")
    s_side_g = swap(s_side)

    keep, send = call(
        large_body,
        [((32, 8, 128), F32)] * 2,
        (where, kept, taken, maps, maps_g, all_l, k_side, k_side_g, k_far, k_far_g),
        [pltpu.VMEM((256, 4096), F32), pltpu.VMEM((512, HD), BF)],
        flops=2**32,
    )
    keep, send, s_far = tie(keep, send, s_far)
    got = swap(send)
    s_far_g = swap(s_far)
    (total,) = call(
        small_body,
        [((32, 8, 128), F32)],
        (where, query_s, maps, maps_g, keep, got, all_s, s_side, s_side_g, s_far, s_far_g),
        [pltpu.VMEM((128, 4096), F32)],
        flops=2**30,
    )

    returned = lax.all_to_all(total, ("z", "x"), split_axis=0, concat_axis=0, tiled=True)
    returned = jnp.sum(returned, axis=0)
    latent_l = lax.dynamic_slice_in_dim(latent_large, core * 16, 16, 0)
    latent_s = lax.dynamic_slice_in_dim(latent_small, core * 16, 16, 0)
    direct = GUIDANCE * jnp.dot(latent_l, head_large, preferred_element_type=F32) + (
        1.0 - GUIDANCE
    ) * jnp.dot(latent_s, head_small, preferred_element_type=F32)
    part = direct + jnp.concatenate([returned[:, :64], returned[:, 64:]], 0)
    other_part = swap(part)
    return jnp.where(
        core == 0,
        jnp.concatenate([part, other_part], 0),
        jnp.concatenate([other_part, part], 0),
    )


def solution(mesh):
    grid = Mesh(mesh.devices.reshape(2, 8, 4, 4), ("grp", "z", "x", "y"))
    tokens = ("z", "x", "y")
    return jax.shard_map(
        shards,
        mesh=grid,
        in_specs=(
            P(tokens, None),
            P(tokens, None),
            P(),
            P(),
            P(None, ("grp",) + tokens),
            P(None, ("grp",) + tokens),
            P("grp", None),
            P("grp", None),
            P(),
            P(),
        ),
        out_specs=P(tokens, None),
        check_vma=False,
    )
```

```python
import jax
import jax.numpy as jnp
from jax import lax
from jax.experimental import pallas as pl
from jax.experimental.pallas import tpu as pltpu
from jax.sharding import Mesh, PartitionSpec as P

HD = 128
GUIDANCE = 3.0
EPSILON = 1e-06
BF = jnp.bfloat16
F32 = jnp.float32
DL, DS = 5120, 1536
KS = DS // 2
PART = 512
LOG2E = 1.4426950408889634
VMEM = pl.BlockSpec(memory_space=pltpu.VMEM)
SMEM = pl.BlockSpec(memory_space=pltpu.SMEM)
ANY = pl.BlockSpec(memory_space=pl.ANY)
OPPOSITE = [(0, 3), (3, 0), (1, 2), (2, 1)]


def flip(block, axis, mask):
    count = lax.axis_size(axis)
    return lax.ppermute(block, axis, [(i, i ^ mask) for i in range(count)])


def swap(block):
    return flip(block, "grp", 1)


def cross(block):
    return lax.ppermute(block, "x", OPPOSITE)


def spread(block, axis):
    n = lax.axis_size(axis)
    pairs = [(i, (i + 1) % n) for i in range(n)]
    pairs += [(n + i, n + (i - 1) % n) for i in range(n)]
    return lax.ppermute(block, ("grp", axis), pairs)


def tie(*values):
    return lax.optimization_barrier(values)


def dot_t(rows, columns):
    return lax.dot_general(
        rows, columns, (((1,), (1,)), ((), ())), preferred_element_type=F32
    )


def call(body, outs, args, scratch=(), limit=16, placed=None, flops=0):
    return pl.pallas_call(
        body,
        out_shape=[jax.ShapeDtypeStruct(shape, dtype) for shape, dtype in outs],
        in_specs=placed or [SMEM] + [VMEM] * (len(args) - 1),
        out_specs=[VMEM] * len(outs),
        scratch_shapes=list(scratch),
        compiler_params=pltpu.CompilerParams(vmem_limit_bytes=limit * 2**20),
        cost_estimate=pl.CostEstimate(flops=flops, bytes_accessed=2**20, transcendentals=0),
    )(*args)


def pack(shape, pieces):
    def body(*refs):
        sources, out, sems = refs[: len(pieces)], refs[-2], refs[-1]
        tasks = []
        for i, (source, (_, part, to)) in enumerate(zip(sources, pieces)):
            source = source if part is None else source.at[part]
            tasks.append(pltpu.make_async_copy(source, out.at[to], sems.at[i]))
        for task in tasks:
            task.start()
        for task in tasks:
            task.wait()

    return pl.pallas_call(
        body,
        out_shape=jax.ShapeDtypeStruct(shape, BF),
        in_specs=[ANY] * len(pieces),
        out_specs=ANY,
        scratch_shapes=[pltpu.SemaphoreType.DMA((len(pieces),))],
        compiler_params=pltpu.CompilerParams(vmem_limit_bytes=2**20),
    )(*[piece[0] for piece in pieces])


def norm_body(
    large, small, gain_l, gain_s, mine, other, out_s, hold_l, hold_s, g_l, g_s, sems
):
    core = lax.axis_index("grp")
    tasks = [
        pltpu.make_async_copy(source, target, sems.at[i])
        for i, (source, target) in enumerate(
            ((large, hold_l), (small, hold_s), (gain_l, g_l), (gain_s, g_s))
        )
    ]
    for task in tasks:
        task.start()
    for task in tasks:
        task.wait()

    def normed(latent, gain, half, width):
        values = latent[pl.ds(pl.multiple_of(half * 16, 16), 16), :].astype(F32)
        mean = jnp.mean(values * values, axis=-1, keepdims=True)
        return (values * lax.rsqrt(mean + EPSILON) * gain[...].reshape(1, width)).astype(BF)

    mine[...] = normed(hold_l, g_l, core, DL)
    other[...] = normed(hold_l, g_l, 1 - core, DL)
    for at, half in ((0, core), (32, 1 - core)):
        value = normed(hold_s, g_s, half, DS)
        out_s[at : at + 16, :] = value[:, :KS]
        out_s[at + 16 : at + 32, :] = value[:, KS:]


def ordered(value, order):
    return lax.dot_general(
        value, order[...], (((0,), (0,)), ((), ())), preferred_element_type=F32
    ).astype(BF)


def setup_body(where, mix_l, mix_s, order_l, order_s, maps):
    core, z, x, y = (where[i] for i in range(4))
    x_low, z_low = x % 2, z % 2

    def position(y_at):
        away = (y - y_at) & 3
        return jnp.where((away & 1 == 1) & (core == 1), 4 - away, away)

    def lines(size, axis):
        return lax.broadcasted_iota(jnp.int32, (1, size) if axis else (size, 1), axis)

    target = lines(384, 1)
    block = target // 48
    base = jnp.where(block // 4 == x_low, 0, 4) + position(block & 3)
    order_l[...] = (lines(384, 0) == base * 48 + target % 48).astype(F32).astype(BF)

    half = target // 192
    group = jnp.where((half == z_low) == (core == z_low), 0, 1)
    within = target % 192
    piece = within // 12
    mask = (piece // 4) ^ x
    side = jnp.where(mask == 3, 1, jnp.where(mask == 1, 2, jnp.where(mask == 2, 3, 0)))
    base = (group * 16 + position(piece & 3) * 4 + side) * 16 + within % 12
    order_s[...] = (lines(512, 0) == base).astype(F32).astype(BF)

    maps[:64, :] = mix_l[:, pl.ds(pl.multiple_of((z * 2 + x // 2) * HD, HD), HD)]
    maps[64:, :] = mix_s[:, pl.ds(pl.multiple_of(z // 2 * HD, HD), HD)]


def sides(mine, own, other):
    rows = jnp.where(mine, own, other)
    blank = jnp.zeros_like(rows)
    return jnp.concatenate([rows, blank], 0), jnp.concatenate([blank, rows], 0)


def project_small_body(
    where, own, s1, z1, z2, z3, got, ws, ws_g, yz, yz_g, far, far_g, order, query, pairs, rows
):
    core, z = where[0], where[1]
    way = 2 * core - 1

    def put(step, ref, row, col):
        at = pl.ds(pl.multiple_of((z + 8 + step) % 8 * 16, 16), 16)
        rows[at, :KS] = ref[row : row + 16, col:]
        rows[at, KS:] = ref[row + 16 : row + 32, col:]

    put(0, own, 0, 0)
    put(4, z3, 0, DL)
    for i, ref, col in ((1, s1, 0), (2, z1, DL), (3, z2, DL)):
        put(way * i, ref, 0, col)
        put(-way * i, got, 32 * i - 32, 0)

    blocks = (
        (ws, 0), (yz, 2 * DL), (far, 0), (yz_g, 2 * DL + 4 * PART),
        (ws_g, 0), (yz, 2 * DL + 4 * PART), (far_g, 0), (yz_g, 2 * DL),
    )
    small = None
    for q in range(3):
        cols = jnp.concatenate(
            [
                ref[16 * q : 16 * q + 16, col + PART * side : col + PART * side + PART]
                for ref, col in blocks
                for side in range(4)
            ],
            0,
        )
        term = dot_t(cols, rows[:, PART * q : PART * q + PART])
        small = term if small is None else small + term
    small = ordered(small.astype(BF), order)
    query[...] = small[:, :HD]
    pairs[...] = small[:, HD:]


def project_body(
    where, near, z1, z2, z3, z4, w0, y1, y1_g, yz, pr, y2, y2_g, own, other
):
    blocks = (
        (w0, 0, 0), (y1, 0, 0), (yz, 0, 0), (y1_g, 48, 0),
        (pr, 0, 0), (y2, 0, 0), (yz, 0, DL), (y2_g, 48, 0),
        (w0, 48, 0), (y1, 48, 0), (y1_g, 0, 0), (pr, 48, 0), (y2, 48, 0), (y2_g, 0, 0),
    )
    total = product(blocks, (near, z1, z2, z3, z4))
    own[...] = total[:384, :]
    other[...] = total[384:, :]


def product(blocks, rows):
    near, z1, z2, z3, z4 = rows
    total = None
    for k in range(0, DL, 1024):
        at = slice(k, k + 1024)
        cols = jnp.concatenate(
            [ref[row : row + 48, col + k : col + k + 1024] for ref, row, col in blocks], 0
        )
        parts = [near[:, at], z1[:, at], z2[32:, at], z2[:32, at], z3[32:, at]]
        parts += [z3[:32, at], z4[32:, at], z4[:32, at]]
        term = dot_t(cols, jnp.concatenate(parts, 0))
        total = term if total is None else total + term
    return total.astype(BF)


def finish_body(where, near, z1, z2, z3, z4, yz_g, own, other, order, kept, sent):
    core, x = where[0], where[2]
    far = product(((yz_g, 0, 0), (yz_g, 0, DL)), (near, z1, z2, z3, z4))
    parts = [other[0:96, :], far[:48, :], other[96:240, :], far[48:, :], other[240:, :]]
    first, second = own[...], jnp.concatenate(parts, 0)
    mine = core == x % 2
    sent[...] = ordered(jnp.where(mine, second, first), order)
    kept[...] = ordered(jnp.where(mine, first, second), order)


def attend(query, pairs, scores):
    top = None
    start = 0
    for ref, first, last in pairs:
        for lo in range(first, last, 512):
            count = 512
            block = dot_t(query, ref[lo : lo + count, :HD])
            scores[:, start : start + count] = block
            for at in range(0, count, 128):
                part = block[:, at : at + 128]
                top = part if top is None else jnp.maximum(top, part)
            start += count
    biggest = jnp.max(top, axis=1, keepdims=True)
    total, mixed = None, None
    start = 0
    for ref, first, last in pairs:
        for lo in range(first, last, 512):
            count = 512
            block = scores[:, start : start + count]
            weights = jnp.exp2((block - biggest) * (HD**-0.5 * LOG2E))
            for at in range(0, count, 128):
                part = weights[:, at : at + 128]
                total = part if total is None else total + part
            values = ref[lo : lo + count, HD:]
            term = jnp.dot(weights.astype(BF), values, preferred_element_type=F32)
            mixed = term if mixed is None else mixed + term
            start += count
    return (mixed / jnp.sum(total, axis=1, keepdims=True)).astype(BF)


def large_body(
    where, kept, taken, maps, maps_g, own, side, side_g, far, far_g,
    keep, send, scores, query,
):
    pairs = ((own, 0, 1024), (side, 0, 1024), (side_g, 0, 1024), (far, 0, 512), (far_g, 0, 512))
    core, z, x = where[0], where[1], where[2]
    way = 2 * core - 1
    keep[...] = jnp.zeros_like(keep)
    send[...] = jnp.zeros_like(send)
    query[:256, :] = kept[:, :HD]
    query[256:, :] = taken[:, :HD]
    map_left, map_right = sides(core == x % 2, maps[:64, :], maps_g[:64, :])

    @pl.loop(0, 2)
    def _(s):
        done = attend(query[pl.ds(pl.multiple_of(s * 256, 256), 256), :], pairs, scores)
        left = GUIDANCE * dot_t(done, map_left)
        right = GUIDANCE * dot_t(done, map_right)
        x_own = x ^ s

        def chip(step, x_at):
            return (z + 8 + step) % 8 * 4 + x_at

        def folded(row):
            return left[row : row + 8] + right[row + 8 : row + 16]

        for step, row in ((0, 0), (4, 224)) + tuple((way * i, 64 * i - 32) for i in (1, 2, 3)):
            keep[chip(step, x_own)] = folded(row)
            keep[chip(step, x_own ^ 3)] = folded(row + 16)
        for i in (1, 2, 3):
            send[chip(way * i, x_own)] = folded(64 * i)
            send[chip(way * i, x_own ^ 3)] = folded(64 * i + 16)


def small_body(
    where, query, maps, maps_g, keep, got, own, side, side_g, far, far_g, out, scores
):
    pairs = ((own, 0, 1024), (side, 0, 1024), (side_g, 0, 1024), (far, 0, 512), (far_g, 0, 512))
    core, z_at, x = where[0], where[1], where[2]
    map_left, map_right = sides(core == z_at % 2, maps[64:, :], maps_g[64:, :])
    done = attend(query[...], pairs, scores)
    left = (1.0 - GUIDANCE) * dot_t(done, map_left)
    right = (1.0 - GUIDANCE) * dot_t(done, map_right)
    out[...] = keep[...] + got[...]
    for z in range(8):
        out[z * 4 + x] += left[16 * z : 16 * z + 8] + right[16 * z + 8 : 16 * z + 16]


def shards(
    latent_large,
    latent_small,
    gain_large,
    gain_small,
    qkv_large,
    qkv_small,
    mix_large,
    mix_small,
    head_large,
    head_small,
):
    core, z, x, y = (lax.axis_index(name) for name in ("grp", "z", "x", "y"))
    x_low, z_low = x & 1, z & 1
    where = jnp.stack([core, z, x, y])

    mine, other, s0 = call(
        norm_body,
        [((16, DL), BF), ((16, DL), BF), ((64, KS), BF)],
        (latent_large, latent_small, gain_large, gain_small),
        [
            pltpu.VMEM((32, DL), BF),
            pltpu.VMEM((32, DS), BF),
            pltpu.VMEM((DL,), F32),
            pltpu.VMEM((DS,), F32),
            pltpu.SemaphoreType.DMA((4,)),
        ],
        limit=60,
        placed=[ANY] * 4,
    )
    w, ws = qkv_large.T, qkv_small.T
    w_g = swap(w)
    xw = flip(w, "x", 1)
    across = cross(mine)
    s1 = spread(s0, "z")
    w_g, ws, mix_l, mix_s, _ = tie(w_g, ws, mix_large.T, mix_small.T, mine)
    top, low, left, right = slice(0, 48), slice(48, 96), slice(0, DL), slice(DL, None)
    near, pair, every = slice(0, 16), slice(16, 32), slice(None)
    ws = jnp.concatenate([ws, jnp.zeros((4, DS), BF)], 0)
    ws = jnp.concatenate([ws[:, :PART], ws[:, PART : 2 * PART], ws[:, 2 * PART :]], 0)
    trade = [(g * 8 + i, (1 - g) * 8 + (i ^ 1)) for g in range(2) for i in range(8) if i % 2 != g]
    ws_other = lax.ppermute(ws, ("grp", "z"), trade)
    w0 = pack((96, DL), [(w, None, top), (w_g, None, low)])
    y1 = spread(w0, "y")
    order_l, order_s, maps = call(
        setup_body,
        [((384, 384), BF), ((512, 384), BF), ((HD, HD), BF)],
        (where, mix_l, mix_s),
    )

    across, s1, w0, ws_other = tie(across, s1, w0, ws_other)
    ws = jnp.where(core == z_low, ws, ws_other)
    ws_cross = cross(ws)

    def block(at, own, facing, small):
        return [
            (own, None, (slice(at, at + 16), left)),
            (facing, None, (slice(at + 16, at + 32), left)),
            (s1, small, (slice(at, at + 32), right)),
        ]

    a0 = pack((32, DL + KS), block(0, mine, across, slice(0, 32)))
    z1 = spread(a0, "z")
    across, xw, _ = tie(across, xw, a0)
    got = swap(across)
    pr = pack((96, DL), [(xw, None, top), (swap(xw), None, low)])

    z1, y1, got, pr, ws_cross, maps = tie(z1, y1, got, pr, ws_cross, maps)
    z2 = spread(
        pack((64, DL + KS), [(z1, None, slice(0, 32))] + block(32, other, got, slice(32, 64))), "z"
    )
    y2 = spread(pr, "y")
    ws2 = jnp.concatenate([ws, ws_cross], 1)
    ws4 = jnp.concatenate([ws2, flip(ws2, "x", 1)], 1)
    ws4_g = swap(ws4)
    y1_g = swap(y1)
    maps_g = swap(maps)

    z2, y1, y1_g, y2, ws4, ws4_g, maps_g = tie(z2, y1, y1_g, y2, ws4, ws4_g, maps_g)
    z3 = spread(z2, "z")
    ends = [slice(DL, 2 * DL), slice(2 * DL, 2 * DL + 4 * PART), slice(2 * DL + 4 * PART, None)]
    yz = spread(
        pack(
            (48, 2 * DL + 8 * PART),
            [(y1, top, (every, left)), (y2, top, (every, ends[0]))]
            + [(ws4, None, (every, ends[1])), (ws4_g, None, (every, ends[2]))],
        ),
        "y",
    )
    y2_g = swap(y2)

    z3, y2_g = tie(z3, y2_g)
    z4 = spread(z3, "z")
    s_got = swap(
        pack(
            (96, KS),
            [
                (s1, slice(32, 64), slice(0, 32)),
                (z2, (slice(32, 64), right), slice(32, 64)),
                (z3, (slice(32, 64), right), slice(64, 96)),
            ],
        )
    )

    z4, yz, s_got = tie(z4, yz, s_got)
    far_s = spread(pack((48, 4 * PART), [(yz, (every, ends[1]), every)]), "y")
    yz_g = swap(yz)
    own, another = call(
        project_body,
        [((384, 256), BF), ((288, 256), BF)],
        (where, a0, z1, z2, z3, z4, w0, y1, y1_g, yz, pr, y2, y2_g),
        limit=12,
        flops=2**32,
    )
    kept, sent = call(
        finish_body,
        [((256, 384), BF)] * 2,
        (where, a0, z1, z2, z3, z4, yz_g, own, another, order_l),
        limit=12,
        flops=2**29,
    )

    taken = flip(sent, "x", 1)
    kept_g = swap(kept)
    far_s, _ = tie(far_s, sent)
    far_s_g = swap(far_s)
    query_s, own_s = call(
        project_small_body,
        [((128, HD), BF), ((128, 2 * HD), BF)],
        (where, s0, s1, z1, z2, z3, s_got, ws4, ws4_g, yz, yz_g, far_s, far_s_g, order_s),
        [pltpu.VMEM((128, DS), BF)],
        limit=6,
        flops=2**29,
    )
    got_s = swap(own_s)
    taken, got_s = tie(taken, got_s)
    x1 = spread(jnp.concatenate([own_s, got_s], 0), "x")
    x2 = flip(own_s, "x", 2)

    pairs = slice(HD, None)
    taken_g = swap(taken)
    all_l = pack(
        (1024, 2 * HD),
        [
            (value, (every, pairs), slice(256 * i, 256 * i + 256))
            for i, value in enumerate((kept, taken, kept_g, taken_g))
        ],
    )
    k_side = spread(all_l, "y")

    x1_g, x2_g = swap(x1), swap(x2)
    first, second = slice(0, 128), slice(128, 256)
    parts = ((own_s, None), (x1, first), (x1_g, second), (x2, None))
    parts += ((got_s, None), (x1, second), (x1_g, first), (x2_g, None))
    all_s = pack(
        (1024, 2 * HD),
        [(value, part, slice(128 * i, 128 * i + 128)) for i, (value, part) in enumerate(parts)],
    )
    s_side = spread(all_s, "y")
    k_side, _ = tie(k_side, all_s)
    k_far = spread(k_side[:512], "y")
    k_side_g = swap(k_side)
    k_far, _ = tie(k_far, s_side)
    k_far_g = swap(k_far)
    s_far = spread(s_side[:512], "y")
    s_side_g = swap(s_side)

    keep, send = call(
        large_body,
        [((32, 8, 128), F32)] * 2,
        (where, kept, taken, maps, maps_g, all_l, k_side, k_side_g, k_far, k_far_g),
        [pltpu.VMEM((256, 4096), F32), pltpu.VMEM((512, HD), BF)],
        flops=2**32,
    )
    keep, send, s_far = tie(keep, send, s_far)
    got = swap(send)
    s_far_g = swap(s_far)
    (total,) = call(
        small_body,
        [((32, 8, 128), F32)],
        (where, query_s, maps, maps_g, keep, got, all_s, s_side, s_side_g, s_far, s_far_g),
        [pltpu.VMEM((128, 4096), F32)],
        flops=2**30,
    )

    returned = lax.all_to_all(total, ("z", "x"), split_axis=0, concat_axis=0, tiled=True)
    returned = jnp.sum(returned, axis=0)
    latent_l = lax.dynamic_slice_in_dim(latent_large, core * 16, 16, 0)
    latent_s = lax.dynamic_slice_in_dim(latent_small, core * 16, 16, 0)
    direct = GUIDANCE * jnp.dot(latent_l, head_large, preferred_element_type=F32) + (
        1.0 - GUIDANCE
    ) * jnp.dot(latent_s, head_small, preferred_element_type=F32)
    part = direct + jnp.concatenate([returned[:, :64], returned[:, 64:]], 0)
    other_part = swap(part)
    return jnp.where(
        core == 0,
        jnp.concatenate([part, other_part], 0),
        jnp.concatenate([other_part, part], 0),
    )


def solution(mesh):
    grid = Mesh(mesh.devices.reshape(2, 8, 4, 4), ("grp", "z", "x", "y"))
    tokens = ("z", "x", "y")
    return jax.shard_map(
        shards,
        mesh=grid,
        in_specs=(
            P(tokens, None),
            P(tokens, None),
            P(),
            P(),
            P(None, ("grp",) + tokens),
            P(None, ("grp",) + tokens),
            P("grp", None),
            P("grp", None),
            P(),
            P(),
        ),
        out_specs=P(tokens, None),
        check_vma=False,
    )
```

```python
import jax
import jax.numpy as jnp
from jax import lax
from jax.experimental import pallas as pl
from jax.experimental.pallas import tpu as pltpu
from jax.sharding import Mesh, PartitionSpec as P

HD = 128
GUIDANCE = 3.0
EPSILON = 1e-06
BF = jnp.bfloat16
F32 = jnp.float32
DL, DS = 5120, 1536
KS = DS // 2
PART = 512
LOG2E = 1.4426950408889634
VMEM = pl.BlockSpec(memory_space=pltpu.VMEM)
SMEM = pl.BlockSpec(memory_space=pltpu.SMEM)
ANY = pl.BlockSpec(memory_space=pl.ANY)
OPPOSITE = [(0, 3), (3, 0), (1, 2), (2, 1)]


def flip(block, axis, mask):
    count = lax.axis_size(axis)
    return lax.ppermute(block, axis, [(i, i ^ mask) for i in range(count)])


def swap(block):
    return flip(block, "grp", 1)


def cross(block):
    return lax.ppermute(block, "x", OPPOSITE)


def spread(block, axis):
    n = lax.axis_size(axis)
    pairs = [(i, (i + 1) % n) for i in range(n)]
    pairs += [(n + i, n + (i - 1) % n) for i in range(n)]
    return lax.ppermute(block, ("grp", axis), pairs)


def tie(*values):
    return lax.optimization_barrier(values)


def dot_t(rows, columns):
    return lax.dot_general(
        rows, columns, (((1,), (1,)), ((), ())), preferred_element_type=F32
    )


def call(body, outs, args, scratch=(), limit=16, placed=None, flops=0):
    return pl.pallas_call(
        body,
        out_shape=[jax.ShapeDtypeStruct(shape, dtype) for shape, dtype in outs],
        in_specs=placed or [SMEM] + [VMEM] * (len(args) - 1),
        out_specs=[VMEM] * len(outs),
        scratch_shapes=list(scratch),
        compiler_params=pltpu.CompilerParams(vmem_limit_bytes=limit * 2**20),
        cost_estimate=pl.CostEstimate(flops=flops, bytes_accessed=2**20, transcendentals=0),
    )(*args)


def pack(shape, pieces):
    def body(*refs):
        sources, out, sems = refs[: len(pieces)], refs[-2], refs[-1]
        tasks = []
        for i, (source, (_, part, to)) in enumerate(zip(sources, pieces)):
            source = source if part is None else source.at[part]
            tasks.append(pltpu.make_async_copy(source, out.at[to], sems.at[i]))
        for task in tasks:
            task.start()
        for task in tasks:
            task.wait()

    return pl.pallas_call(
        body,
        out_shape=jax.ShapeDtypeStruct(shape, BF),
        in_specs=[ANY] * len(pieces),
        out_specs=ANY,
        scratch_shapes=[pltpu.SemaphoreType.DMA((len(pieces),))],
        compiler_params=pltpu.CompilerParams(vmem_limit_bytes=2**20),
    )(*[piece[0] for piece in pieces])


def norm_body(
    large, small, gain_l, gain_s, mine, other, out_s, hold_l, hold_s, g_l, g_s, sems
):
    core = lax.axis_index("grp")
    tasks = [
        pltpu.make_async_copy(source, target, sems.at[i])
        for i, (source, target) in enumerate(
            ((large, hold_l), (small, hold_s), (gain_l, g_l), (gain_s, g_s))
        )
    ]
    for task in tasks:
        task.start()
    for task in tasks:
        task.wait()

    def normed(latent, gain, half, width):
        values = latent[pl.ds(pl.multiple_of(half * 16, 16), 16), :].astype(F32)
        mean = jnp.mean(values * values, axis=-1, keepdims=True)
        return (values * lax.rsqrt(mean + EPSILON) * gain[...].reshape(1, width)).astype(BF)

    mine[...] = normed(hold_l, g_l, core, DL)
    other[...] = normed(hold_l, g_l, 1 - core, DL)
    for at, half in ((0, core), (32, 1 - core)):
        value = normed(hold_s, g_s, half, DS)
        out_s[at : at + 16, :] = value[:, :KS]
        out_s[at + 16 : at + 32, :] = value[:, KS:]


def ordered(value, order):
    return lax.dot_general(
        value, order[...], (((0,), (0,)), ((), ())), preferred_element_type=F32
    ).astype(BF)


def setup_body(where, mix_l, mix_s, order_l, order_s, maps):
    core, z, x, y = (where[i] for i in range(4))
    x_low, z_low = x % 2, z % 2

    def position(y_at):
        away = (y - y_at) & 3
        return jnp.where((away & 1 == 1) & (core == 1), 4 - away, away)

    def lines(size, axis):
        return lax.broadcasted_iota(jnp.int32, (1, size) if axis else (size, 1), axis)

    target = lines(384, 1)
    block = target // 48
    base = jnp.where(block // 4 == x_low, 0, 4) + position(block & 3)
    order_l[...] = (lines(384, 0) == base * 48 + target % 48).astype(F32).astype(BF)

    half = target // 192
    group = jnp.where((half == z_low) == (core == z_low), 0, 1)
    within = target % 192
    piece = within // 12
    mask = (piece // 4) ^ x
    side = jnp.where(mask == 3, 1, jnp.where(mask == 1, 2, jnp.where(mask == 2, 3, 0)))
    base = (group * 16 + position(piece & 3) * 4 + side) * 16 + within % 12
    order_s[...] = (lines(512, 0) == base).astype(F32).astype(BF)

    maps[:64, :] = mix_l[:, pl.ds(pl.multiple_of((z * 2 + x // 2) * HD, HD), HD)]
    maps[64:, :] = mix_s[:, pl.ds(pl.multiple_of(z // 2 * HD, HD), HD)]


def sides(mine, own, other):
    rows = jnp.where(mine, own, other)
    blank = jnp.zeros_like(rows)
    return jnp.concatenate([rows, blank], 0), jnp.concatenate([blank, rows], 0)


def project_small_body(
    where, own, s1, z1, z2, z3, got, ws, ws_g, yz, yz_g, far, far_g, order, query, pairs, rows
):
    core, z = where[0], where[1]
    way = 2 * core - 1

    def put(step, ref, row, col):
        at = pl.ds(pl.multiple_of((z + 8 + step) % 8 * 16, 16), 16)
        rows[at, :KS] = ref[row : row + 16, col:]
        rows[at, KS:] = ref[row + 16 : row + 32, col:]

    put(0, own, 0, 0)
    put(4, z3, 0, DL)
    for i, ref, col in ((1, s1, 0), (2, z1, DL), (3, z2, DL)):
        put(way * i, ref, 0, col)
        put(-way * i, got, 32 * i - 32, 0)

    blocks = (
        (ws, 0), (yz, 2 * DL), (far, 0), (yz_g, 2 * DL + 4 * PART),
        (ws_g, 0), (yz, 2 * DL + 4 * PART), (far_g, 0), (yz_g, 2 * DL),
    )
    small = None
    for q in range(3):
        cols = jnp.concatenate(
            [
                ref[16 * q : 16 * q + 16, col + PART * side : col + PART * side + PART]
                for ref, col in blocks
                for side in range(4)
            ],
            0,
        )
        term = dot_t(cols, rows[:, PART * q : PART * q + PART])
        small = term if small is None else small + term
    small = ordered(small.astype(BF), order)
    query[...] = small[:, :HD]
    pairs[...] = small[:, HD:]


def project_body(
    where, near, z1, z2, z3, z4, w0, y1, y1_g, yz, pr, y2, y2_g, own, other
):
    blocks = (
        (w0, 0, 0), (y1, 0, 0), (yz, 0, 0), (y1_g, 48, 0),
        (pr, 0, 0), (y2, 0, 0), (yz, 0, DL), (y2_g, 48, 0),
        (w0, 48, 0), (y1, 48, 0), (y1_g, 0, 0), (pr, 48, 0), (y2, 48, 0), (y2_g, 0, 0),
    )
    total = product(blocks, (near, z1, z2, z3, z4))
    own[...] = total[:384, :]
    other[...] = total[384:, :]


def product(blocks, rows):
    near, z1, z2, z3, z4 = rows
    total = None
    for k in range(0, DL, 1024):
        at = slice(k, k + 1024)
        cols = jnp.concatenate(
            [ref[row : row + 48, col + k : col + k + 1024] for ref, row, col in blocks], 0
        )
        parts = [near[:, at], z1[:, at], z2[32:, at], z2[:32, at], z3[32:, at]]
        parts += [z3[:32, at], z4[32:, at], z4[:32, at]]
        term = dot_t(cols, jnp.concatenate(parts, 0))
        total = term if total is None else total + term
    return total.astype(BF)


def finish_body(where, near, z1, z2, z3, z4, yz_g, own, other, order, kept, sent):
    core, x = where[0], where[2]
    far = product(((yz_g, 0, 0), (yz_g, 0, DL)), (near, z1, z2, z3, z4))
    parts = [other[0:96, :], far[:48, :], other[96:240, :], far[48:, :], other[240:, :]]
    first, second = own[...], jnp.concatenate(parts, 0)
    mine = core == x % 2
    sent[...] = ordered(jnp.where(mine, second, first), order)
    kept[...] = ordered(jnp.where(mine, first, second), order)


def spots(pairs):
    return [(ref, lo) for ref, first, last in pairs for lo in range(first, last, 512)]


def score(query, spot, scores, start, top):
    ref, lo = spot
    block = dot_t(query, ref[lo : lo + 512, :HD])
    scores[:, start : start + 512] = block
    for at in range(0, 512, 128):
        part = block[:, at : at + 128]
        top = part if top is None else jnp.maximum(top, part)
    return top


def weigh(spot, scores, start, biggest, total, mixed):
    ref, lo = spot
    block = scores[:, start : start + 512]
    weights = jnp.exp2((block - biggest) * (HD**-0.5 * LOG2E))
    for at in range(0, 512, 128):
        part = weights[:, at : at + 128]
        total = part if total is None else total + part
    term = jnp.dot(weights.astype(BF), ref[lo : lo + 512, HD:], preferred_element_type=F32)
    return total, term if mixed is None else mixed + term


def attend(tiles, pairs, scores):
    places = spots(pairs)
    tops = [None] * len(tiles)
    for i, spot in enumerate(places):
        tops[0] = score(tiles[0], spot, scores[0], 512 * i, tops[0])
    done = []
    for t in range(len(tiles)):
        biggest = jnp.max(tops[t], axis=1, keepdims=True)
        total, mixed = None, None
        for i, spot in enumerate(places):
            total, mixed = weigh(spot, scores[t], 512 * i, biggest, total, mixed)
            if t + 1 < len(tiles):
                tops[t + 1] = score(tiles[t + 1], spot, scores[t + 1], 512 * i, tops[t + 1])
        done.append((mixed / jnp.sum(total, axis=1, keepdims=True)).astype(BF))
    return done


def large_body(
    where, kept, taken, maps, maps_g, own, side, side_g, far, far_g,
    keep, send, scores_0, scores_1,
):
    pairs = ((own, 0, 1024), (side, 0, 1024), (side_g, 0, 1024), (far, 0, 512), (far_g, 0, 512))
    core, z, x = where[0], where[1], where[2]
    way = 2 * core - 1
    keep[...] = jnp.zeros_like(keep)
    send[...] = jnp.zeros_like(send)
    map_left, map_right = sides(core == x % 2, maps[:64, :], maps_g[:64, :])

    tiles = attend((kept[:, :HD], taken[:, :HD]), pairs, (scores_0, scores_1))

    def chip(step, x_at):
        return (z + 8 + step) % 8 * 4 + x_at

    for s, done in enumerate(tiles):
        left = GUIDANCE * dot_t(done, map_left)
        right = GUIDANCE * dot_t(done, map_right)
        x_own = x ^ s

        def folded(row):
            return left[row : row + 8] + right[row + 8 : row + 16]

        for step, row in ((0, 0), (4, 224)) + tuple((way * i, 64 * i - 32) for i in (1, 2, 3)):
            keep[chip(step, x_own)] = folded(row)
            keep[chip(step, x_own ^ 3)] = folded(row + 16)
        for i in (1, 2, 3):
            send[chip(way * i, x_own)] = folded(64 * i)
            send[chip(way * i, x_own ^ 3)] = folded(64 * i + 16)


def small_body(
    where, query, maps, maps_g, keep, got, own, side, side_g, far, far_g, out, scores
):
    pairs = ((own, 0, 1024), (side, 0, 1024), (side_g, 0, 1024), (far, 0, 512), (far_g, 0, 512))
    core, z_at, x = where[0], where[1], where[2]
    map_left, map_right = sides(core == z_at % 2, maps[64:, :], maps_g[64:, :])
    (done,) = attend((query[...],), pairs, (scores,))
    left = (1.0 - GUIDANCE) * dot_t(done, map_left)
    right = (1.0 - GUIDANCE) * dot_t(done, map_right)
    out[...] = keep[...] + got[...]
    for z in range(8):
        out[z * 4 + x] += left[16 * z : 16 * z + 8] + right[16 * z + 8 : 16 * z + 16]


def shards(
    latent_large,
    latent_small,
    gain_large,
    gain_small,
    qkv_large,
    qkv_small,
    mix_large,
    mix_small,
    head_large,
    head_small,
):
    core, z, x, y = (lax.axis_index(name) for name in ("grp", "z", "x", "y"))
    x_low, z_low = x & 1, z & 1
    where = jnp.stack([core, z, x, y])

    mine, other, s0 = call(
        norm_body,
        [((16, DL), BF), ((16, DL), BF), ((64, KS), BF)],
        (latent_large, latent_small, gain_large, gain_small),
        [
            pltpu.VMEM((32, DL), BF),
            pltpu.VMEM((32, DS), BF),
            pltpu.VMEM((DL,), F32),
            pltpu.VMEM((DS,), F32),
            pltpu.SemaphoreType.DMA((4,)),
        ],
        limit=60,
        placed=[ANY] * 4,
    )
    w, ws = qkv_large.T, qkv_small.T
    w_g = swap(w)
    xw = flip(w, "x", 1)
    across = cross(mine)
    s1 = spread(s0, "z")
    w_g, ws, mix_l, mix_s, _ = tie(w_g, ws, mix_large.T, mix_small.T, mine)
    top, low, left, right = slice(0, 48), slice(48, 96), slice(0, DL), slice(DL, None)
    near, pair, every = slice(0, 16), slice(16, 32), slice(None)
    ws = jnp.concatenate([ws, jnp.zeros((4, DS), BF)], 0)
    ws = jnp.concatenate([ws[:, :PART], ws[:, PART : 2 * PART], ws[:, 2 * PART :]], 0)
    trade = [(g * 8 + i, (1 - g) * 8 + (i ^ 1)) for g in range(2) for i in range(8) if i % 2 != g]
    ws_other = lax.ppermute(ws, ("grp", "z"), trade)
    w0 = pack((96, DL), [(w, None, top), (w_g, None, low)])
    y1 = spread(w0, "y")
    order_l, order_s, maps = call(
        setup_body,
        [((384, 384), BF), ((512, 384), BF), ((HD, HD), BF)],
        (where, mix_l, mix_s),
    )

    across, s1, w0, ws_other = tie(across, s1, w0, ws_other)
    ws = jnp.where(core == z_low, ws, ws_other)
    ws_cross = cross(ws)

    def block(at, own, facing, small):
        return [
            (own, None, (slice(at, at + 16), left)),
            (facing, None, (slice(at + 16, at + 32), left)),
            (s1, small, (slice(at, at + 32), right)),
        ]

    a0 = pack((32, DL + KS), block(0, mine, across, slice(0, 32)))
    z1 = spread(a0, "z")
    across, xw, _ = tie(across, xw, a0)
    got = swap(across)
    pr = pack((96, DL), [(xw, None, top), (swap(xw), None, low)])

    z1, y1, got, pr, ws_cross, maps = tie(z1, y1, got, pr, ws_cross, maps)
    z2 = spread(
        pack((64, DL + KS), [(z1, None, slice(0, 32))] + block(32, other, got, slice(32, 64))), "z"
    )
    y2 = spread(pr, "y")
    ws2 = jnp.concatenate([ws, ws_cross], 1)
    ws4 = jnp.concatenate([ws2, flip(ws2, "x", 1)], 1)
    ws4_g = swap(ws4)
    y1_g = swap(y1)
    maps_g = swap(maps)

    z2, y1, y1_g, y2, ws4, ws4_g, maps_g = tie(z2, y1, y1_g, y2, ws4, ws4_g, maps_g)
    z3 = spread(z2, "z")
    ends = [slice(DL, 2 * DL), slice(2 * DL, 2 * DL + 4 * PART), slice(2 * DL + 4 * PART, None)]
    yz = spread(
        pack(
            (48, 2 * DL + 8 * PART),
            [(y1, top, (every, left)), (y2, top, (every, ends[0]))]
            + [(ws4, None, (every, ends[1])), (ws4_g, None, (every, ends[2]))],
        ),
        "y",
    )
    y2_g = swap(y2)

    z3, y2_g = tie(z3, y2_g)
    z4 = spread(z3, "z")
    s_got = swap(
        pack(
            (96, KS),
            [
                (s1, slice(32, 64), slice(0, 32)),
                (z2, (slice(32, 64), right), slice(32, 64)),
                (z3, (slice(32, 64), right), slice(64, 96)),
            ],
        )
    )

    z4, yz, s_got = tie(z4, yz, s_got)
    far_s = spread(pack((48, 4 * PART), [(yz, (every, ends[1]), every)]), "y")
    yz_g = swap(yz)
    own, another = call(
        project_body,
        [((384, 256), BF), ((288, 256), BF)],
        (where, a0, z1, z2, z3, z4, w0, y1, y1_g, yz, pr, y2, y2_g),
        limit=12,
        flops=2**32,
    )
    kept, sent = call(
        finish_body,
        [((256, 384), BF)] * 2,
        (where, a0, z1, z2, z3, z4, yz_g, own, another, order_l),
        limit=12,
        flops=2**29,
    )

    taken = flip(sent, "x", 1)
    kept_g = swap(kept)
    far_s, _ = tie(far_s, sent)
    far_s_g = swap(far_s)
    query_s, own_s = call(
        project_small_body,
        [((128, HD), BF), ((128, 2 * HD), BF)],
        (where, s0, s1, z1, z2, z3, s_got, ws4, ws4_g, yz, yz_g, far_s, far_s_g, order_s),
        [pltpu.VMEM((128, DS), BF)],
        limit=6,
        flops=2**29,
    )
    got_s = swap(own_s)
    taken, got_s = tie(taken, got_s)
    x1 = spread(jnp.concatenate([own_s, got_s], 0), "x")
    x2 = flip(own_s, "x", 2)

    pairs = slice(HD, None)
    taken_g = swap(taken)
    all_l = pack(
        (1024, 2 * HD),
        [
            (value, (every, pairs), slice(256 * i, 256 * i + 256))
            for i, value in enumerate((kept, taken, kept_g, taken_g))
        ],
    )
    k_side = spread(all_l, "y")

    x1_g, x2_g = swap(x1), swap(x2)
    first, second = slice(0, 128), slice(128, 256)
    parts = ((own_s, None), (x1, first), (x1_g, second), (x2, None))
    parts += ((got_s, None), (x1, second), (x1_g, first), (x2_g, None))
    all_s = pack(
        (1024, 2 * HD),
        [(value, part, slice(128 * i, 128 * i + 128)) for i, (value, part) in enumerate(parts)],
    )
    s_side = spread(all_s, "y")
    k_side, _ = tie(k_side, all_s)
    k_far = spread(k_side[:512], "y")
    k_side_g = swap(k_side)
    k_far, _ = tie(k_far, s_side)
    k_far_g = swap(k_far)
    s_far = spread(s_side[:512], "y")
    s_side_g = swap(s_side)

    keep, send = call(
        large_body,
        [((32, 8, 128), F32)] * 2,
        (where, kept, taken, maps, maps_g, all_l, k_side, k_side_g, k_far, k_far_g),
        [pltpu.VMEM((256, 4096), F32)] * 2,
        flops=2**32,
    )
    keep, send, s_far = tie(keep, send, s_far)
    got = swap(send)
    s_far_g = swap(s_far)
    (total,) = call(
        small_body,
        [((32, 8, 128), F32)],
        (where, query_s, maps, maps_g, keep, got, all_s, s_side, s_side_g, s_far, s_far_g),
        [pltpu.VMEM((128, 4096), F32)],
        flops=2**30,
    )

    returned = lax.all_to_all(total, ("z", "x"), split_axis=0, concat_axis=0, tiled=True)
    returned = jnp.sum(returned, axis=0)
    latent_l = lax.dynamic_slice_in_dim(latent_large, core * 16, 16, 0)
    latent_s = lax.dynamic_slice_in_dim(latent_small, core * 16, 16, 0)
    direct = GUIDANCE * jnp.dot(latent_l, head_large, preferred_element_type=F32) + (
        1.0 - GUIDANCE
    ) * jnp.dot(latent_s, head_small, preferred_element_type=F32)
    part = direct + jnp.concatenate([returned[:, :64], returned[:, 64:]], 0)
    other_part = swap(part)
    return jnp.where(
        core == 0,
        jnp.concatenate([part, other_part], 0),
        jnp.concatenate([other_part, part], 0),
    )


def solution(mesh):
    grid = Mesh(mesh.devices.reshape(2, 8, 4, 4), ("grp", "z", "x", "y"))
    tokens = ("z", "x", "y")
    return jax.shard_map(
        shards,
        mesh=grid,
        in_specs=(
            P(tokens, None),
            P(tokens, None),
            P(),
            P(),
            P(None, ("grp",) + tokens),
            P(None, ("grp",) + tokens),
            P("grp", None),
            P("grp", None),
            P(),
            P(),
        ),
        out_specs=P(tokens, None),
        check_vma=False,
    )
```

```python
import jax
import jax.numpy as jnp
from jax import lax
from jax.experimental import pallas as pl
from jax.experimental.pallas import tpu as pltpu
from jax.sharding import Mesh, PartitionSpec as P

HD = 128
GUIDANCE = 3.0
EPSILON = 1e-06
BF = jnp.bfloat16
F32 = jnp.float32
DL, DS = 5120, 1536
KS = DS // 2
PART = 512
LOG2E = 1.4426950408889634
VMEM = pl.BlockSpec(memory_space=pltpu.VMEM)
SMEM = pl.BlockSpec(memory_space=pltpu.SMEM)
ANY = pl.BlockSpec(memory_space=pl.ANY)
OPPOSITE = [(0, 3), (3, 0), (1, 2), (2, 1)]


def flip(block, axis, mask):
    count = lax.axis_size(axis)
    return lax.ppermute(block, axis, [(i, i ^ mask) for i in range(count)])


def swap(block):
    return flip(block, "grp", 1)


def cross(block):
    return lax.ppermute(block, "x", OPPOSITE)


def spread(block, axis):
    n = lax.axis_size(axis)
    pairs = [(i, (i + 1) % n) for i in range(n)]
    pairs += [(n + i, n + (i - 1) % n) for i in range(n)]
    return lax.ppermute(block, ("grp", axis), pairs)


def tie(*values):
    return lax.optimization_barrier(values)


def dot_t(rows, columns):
    return lax.dot_general(
        rows, columns, (((1,), (1,)), ((), ())), preferred_element_type=F32
    )


def call(body, outs, args, scratch=(), limit=16, placed=None, flops=0):
    return pl.pallas_call(
        body,
        out_shape=[jax.ShapeDtypeStruct(shape, dtype) for shape, dtype in outs],
        in_specs=placed or [SMEM] + [VMEM] * (len(args) - 1),
        out_specs=[VMEM] * len(outs),
        scratch_shapes=list(scratch),
        compiler_params=pltpu.CompilerParams(vmem_limit_bytes=limit * 2**20),
        cost_estimate=pl.CostEstimate(flops=flops, bytes_accessed=2**20, transcendentals=0),
    )(*args)


def pack(shape, pieces):
    def body(*refs):
        sources, out, sems = refs[: len(pieces)], refs[-2], refs[-1]
        tasks = []
        for i, (source, (_, part, to)) in enumerate(zip(sources, pieces)):
            source = source if part is None else source.at[part]
            tasks.append(pltpu.make_async_copy(source, out.at[to], sems.at[i]))
        for task in tasks:
            task.start()
        for task in tasks:
            task.wait()

    return pl.pallas_call(
        body,
        out_shape=jax.ShapeDtypeStruct(shape, BF),
        in_specs=[ANY] * len(pieces),
        out_specs=ANY,
        scratch_shapes=[pltpu.SemaphoreType.DMA((len(pieces),))],
        compiler_params=pltpu.CompilerParams(vmem_limit_bytes=2**20),
    )(*[piece[0] for piece in pieces])


def norm_body(
    large, small, gain_l, gain_s, mine, other, out_s, hold_l, hold_s, g_l, g_s, sems
):
    core = lax.axis_index("grp")
    tasks = [
        pltpu.make_async_copy(source, target, sems.at[i])
        for i, (source, target) in enumerate(
            ((large, hold_l), (small, hold_s), (gain_l, g_l), (gain_s, g_s))
        )
    ]
    for task in tasks:
        task.start()
    for task in tasks:
        task.wait()

    def normed(latent, gain, half, width):
        values = latent[pl.ds(pl.multiple_of(half * 16, 16), 16), :].astype(F32)
        mean = jnp.mean(values * values, axis=-1, keepdims=True)
        return (values * lax.rsqrt(mean + EPSILON) * gain[...].reshape(1, width)).astype(BF)

    mine[...] = normed(hold_l, g_l, core, DL)
    other[...] = normed(hold_l, g_l, 1 - core, DL)
    for at, half in ((0, core), (32, 1 - core)):
        value = normed(hold_s, g_s, half, DS)
        out_s[at : at + 16, :] = value[:, :KS]
        out_s[at + 16 : at + 32, :] = value[:, KS:]


def ordered(value, order):
    return lax.dot_general(
        value, order[...], (((0,), (0,)), ((), ())), preferred_element_type=F32
    ).astype(BF)


def setup_body(where, mix_l, mix_s, order_l, order_s, maps):
    core, z, x, y = (where[i] for i in range(4))
    x_low, z_low = x % 2, z % 2

    def position(y_at):
        away = (y - y_at) & 3
        return jnp.where((away & 1 == 1) & (core == 1), 4 - away, away)

    def lines(size, axis):
        return lax.broadcasted_iota(jnp.int32, (1, size) if axis else (size, 1), axis)

    target = lines(384, 1)
    block = target // 48
    base = jnp.where(block // 4 == x_low, 0, 4) + position(block & 3)
    order_l[...] = (lines(384, 0) == base * 48 + target % 48).astype(F32).astype(BF)

    half = target // 192
    group = jnp.where((half == z_low) == (core == z_low), 0, 1)
    within = target % 192
    piece = within // 12
    mask = (piece // 4) ^ x
    side = jnp.where(mask == 3, 1, jnp.where(mask == 1, 2, jnp.where(mask == 2, 3, 0)))
    base = (group * 16 + position(piece & 3) * 4 + side) * 16 + within % 12
    order_s[...] = (lines(512, 0) == base).astype(F32).astype(BF)

    maps[:64, :] = mix_l[:, pl.ds(pl.multiple_of((z * 2 + x // 2) * HD, HD), HD)]
    maps[64:, :] = mix_s[:, pl.ds(pl.multiple_of(z // 2 * HD, HD), HD)]


def sides(mine, own, other):
    rows = jnp.where(mine, own, other)
    blank = jnp.zeros_like(rows)
    return jnp.concatenate([rows, blank], 0), jnp.concatenate([blank, rows], 0)


def project_small_body(
    where, own, s1, z1, z2, z3, got, ws, ws_g, yz, yz_g, far, far_g, order, query, pairs, rows
):
    core, z = where[0], where[1]
    way = 2 * core - 1

    def put(step, ref, row, col):
        at = pl.ds(pl.multiple_of((z + 8 + step) % 8 * 16, 16), 16)
        rows[at, :KS] = ref[row : row + 16, col:]
        rows[at, KS:] = ref[row + 16 : row + 32, col:]

    put(0, own, 0, 0)
    put(4, z3, 0, DL)
    for i, ref, col in ((1, s1, 0), (2, z1, DL), (3, z2, DL)):
        put(way * i, ref, 0, col)
        put(-way * i, got, 32 * i - 32, 0)

    blocks = (
        (ws, 0), (yz, 2 * DL), (far, 0), (yz_g, 2 * DL + 4 * PART),
        (ws_g, 0), (yz, 2 * DL + 4 * PART), (far_g, 0), (yz_g, 2 * DL),
    )
    small = None
    for q in range(3):
        cols = jnp.concatenate(
            [
                ref[16 * q : 16 * q + 16, col + PART * side : col + PART * side + PART]
                for ref, col in blocks
                for side in range(4)
            ],
            0,
        )
        term = dot_t(cols, rows[:, PART * q : PART * q + PART])
        small = term if small is None else small + term
    small = ordered(small.astype(BF), order)
    query[...] = small[:, :HD]
    pairs[...] = small[:, HD:]


def project_body(
    where, near, z1, z2, z3, z4, w0, y1, y1_g, yz, pr, y2, y2_g, own, other
):
    blocks = (
        (w0, 0, 0), (y1, 0, 0), (yz, 0, 0), (y1_g, 48, 0),
        (pr, 0, 0), (y2, 0, 0), (yz, 0, DL), (y2_g, 48, 0),
        (w0, 48, 0), (y1, 48, 0), (y1_g, 0, 0), (pr, 48, 0), (y2, 48, 0), (y2_g, 0, 0),
    )
    total = product(blocks, (near, z1, z2, z3, z4))
    own[...] = total[:384, :]
    other[...] = total[384:, :]


def product(blocks, rows):
    near, z1, z2, z3, z4 = rows
    total = None
    for k in range(0, DL, 1024):
        at = slice(k, k + 1024)
        cols = jnp.concatenate(
            [ref[row : row + 48, col + k : col + k + 1024] for ref, row, col in blocks], 0
        )
        parts = [near[:, at], z1[:, at], z2[32:, at], z2[:32, at], z3[32:, at]]
        parts += [z3[:32, at], z4[32:, at], z4[:32, at]]
        term = dot_t(cols, jnp.concatenate(parts, 0))
        total = term if total is None else total + term
    return total.astype(BF)


def finish_body(where, near, z1, z2, z3, z4, yz_g, own, other, order, kept, sent):
    core, x = where[0], where[2]
    far = product(((yz_g, 0, 0), (yz_g, 0, DL)), (near, z1, z2, z3, z4))
    parts = [other[0:96, :], far[:48, :], other[96:240, :], far[48:, :], other[240:, :]]
    first, second = own[...], jnp.concatenate(parts, 0)
    mine = core == x % 2
    sent[...] = ordered(jnp.where(mine, second, first), order)
    kept[...] = ordered(jnp.where(mine, first, second), order)


def spots(pairs):
    return [(ref, lo) for ref, first, last in pairs for lo in range(first, last, 512)]


def score(query, spot, scores, start, top):
    ref, lo = spot
    block = dot_t(query, ref[lo : lo + 512, :HD])
    scores[:, start : start + 512] = block
    for at in range(0, 512, 128):
        part = block[:, at : at + 128]
        top = part if top is None else jnp.maximum(top, part)
    return top


def weigh(spot, scores, start, biggest, total, mixed):
    ref, lo = spot
    block = scores[:, start : start + 512]
    weights = jnp.exp2((block - biggest) * (HD**-0.5 * LOG2E))
    for at in range(0, 512, 128):
        part = weights[:, at : at + 128]
        total = part if total is None else total + part
    term = jnp.dot(weights.astype(BF), ref[lo : lo + 512, HD:], preferred_element_type=F32)
    return total, term if mixed is None else mixed + term


def attend(tiles, pairs, scores):
    places = spots(pairs)
    tops = [None] * len(tiles)
    for i, spot in enumerate(places):
        tops[0] = score(tiles[0], spot, scores[0], 512 * i, tops[0])
    done = []
    for t in range(len(tiles)):
        biggest = jnp.max(tops[t], axis=1, keepdims=True)
        total, mixed = None, None
        for i, spot in enumerate(places):
            total, mixed = weigh(spot, scores[t], 512 * i, biggest, total, mixed)
            if t + 1 < len(tiles):
                tops[t + 1] = score(tiles[t + 1], spot, scores[t + 1], 512 * i, tops[t + 1])
        done.append((mixed / jnp.sum(total, axis=1, keepdims=True)).astype(BF))
    return done


def large_body(
    where, kept, taken, maps, maps_g, own, side, side_g, far, far_g,
    keep, send, scores_0, scores_1,
):
    pairs = ((own, 0, 1024), (side, 0, 1024), (side_g, 0, 1024), (far, 0, 512), (far_g, 0, 512))
    core, z, x = where[0], where[1], where[2]
    way = 2 * core - 1
    keep[...] = jnp.zeros_like(keep)
    send[...] = jnp.zeros_like(send)
    map_left, map_right = sides(core == x % 2, maps[:64, :], maps_g[:64, :])

    tiles = attend((kept[:, :HD], taken[:, :HD]), pairs, (scores_0, scores_1))

    def chip(step, x_at):
        return (z + 8 + step) % 8 * 4 + x_at

    for s, done in enumerate(tiles):
        left = GUIDANCE * dot_t(done, map_left)
        right = GUIDANCE * dot_t(done, map_right)
        x_own = x ^ s

        def folded(row):
            return left[row : row + 8] + right[row + 8 : row + 16]

        for step, row in ((0, 0), (4, 224)) + tuple((way * i, 64 * i - 32) for i in (1, 2, 3)):
            keep[chip(step, x_own)] = folded(row)
            keep[chip(step, x_own ^ 3)] = folded(row + 16)
        for i in (1, 2, 3):
            send[chip(way * i, x_own)] = folded(64 * i)
            send[chip(way * i, x_own ^ 3)] = folded(64 * i + 16)


def small_body(
    where, query, maps, maps_g, keep, own, side, side_g, far, far_g, out, scores
):
    pairs = ((own, 0, 1024), (side, 0, 1024), (side_g, 0, 1024), (far, 0, 512), (far_g, 0, 512))
    core, z_at, x = where[0], where[1], where[2]
    map_left, map_right = sides(core == z_at % 2, maps[64:, :], maps_g[64:, :])
    (done,) = attend((query[...],), pairs, (scores,))
    left = (1.0 - GUIDANCE) * dot_t(done, map_left)
    right = (1.0 - GUIDANCE) * dot_t(done, map_right)
    out[...] = keep[...]
    for z in range(8):
        out[z * 4 + x] += left[16 * z : 16 * z + 8] + right[16 * z + 8 : 16 * z + 16]


def shards(
    latent_large,
    latent_small,
    gain_large,
    gain_small,
    qkv_large,
    qkv_small,
    mix_large,
    mix_small,
    head_large,
    head_small,
):
    core, z, x, y = (lax.axis_index(name) for name in ("grp", "z", "x", "y"))
    x_low, z_low = x & 1, z & 1
    where = jnp.stack([core, z, x, y])

    mine, other, s0 = call(
        norm_body,
        [((16, DL), BF), ((16, DL), BF), ((64, KS), BF)],
        (latent_large, latent_small, gain_large, gain_small),
        [
            pltpu.VMEM((32, DL), BF),
            pltpu.VMEM((32, DS), BF),
            pltpu.VMEM((DL,), F32),
            pltpu.VMEM((DS,), F32),
            pltpu.SemaphoreType.DMA((4,)),
        ],
        limit=60,
        placed=[ANY] * 4,
    )
    w, ws = qkv_large.T, qkv_small.T
    w_g = swap(w)
    xw = flip(w, "x", 1)
    across = cross(mine)
    s1 = spread(s0, "z")
    w_g, ws, mix_l, mix_s, _ = tie(w_g, ws, mix_large.T, mix_small.T, mine)
    top, low, left, right = slice(0, 48), slice(48, 96), slice(0, DL), slice(DL, None)
    near, pair, every = slice(0, 16), slice(16, 32), slice(None)
    ws = jnp.concatenate([ws, jnp.zeros((4, DS), BF)], 0)
    ws = jnp.concatenate([ws[:, :PART], ws[:, PART : 2 * PART], ws[:, 2 * PART :]], 0)
    trade = [(g * 8 + i, (1 - g) * 8 + (i ^ 1)) for g in range(2) for i in range(8) if i % 2 != g]
    ws_other = lax.ppermute(ws, ("grp", "z"), trade)
    w0 = pack((96, DL), [(w, None, top), (w_g, None, low)])
    y1 = spread(w0, "y")
    order_l, order_s, maps = call(
        setup_body,
        [((384, 384), BF), ((512, 384), BF), ((HD, HD), BF)],
        (where, mix_l, mix_s),
    )

    across, s1, w0, ws_other = tie(across, s1, w0, ws_other)
    ws = jnp.where(core == z_low, ws, ws_other)
    ws_cross = cross(ws)

    def block(at, own, facing, small):
        return [
            (own, None, (slice(at, at + 16), left)),
            (facing, None, (slice(at + 16, at + 32), left)),
            (s1, small, (slice(at, at + 32), right)),
        ]

    a0 = pack((32, DL + KS), block(0, mine, across, slice(0, 32)))
    z1 = spread(a0, "z")
    across, xw, _ = tie(across, xw, a0)
    got = swap(across)
    pr = pack((96, DL), [(xw, None, top), (swap(xw), None, low)])

    z1, y1, got, pr, ws_cross, maps = tie(z1, y1, got, pr, ws_cross, maps)
    z2 = spread(
        pack((64, DL + KS), [(z1, None, slice(0, 32))] + block(32, other, got, slice(32, 64))), "z"
    )
    y2 = spread(pr, "y")
    ws2 = jnp.concatenate([ws, ws_cross], 1)
    ws4 = jnp.concatenate([ws2, flip(ws2, "x", 1)], 1)
    ws4_g = swap(ws4)
    y1_g = swap(y1)
    maps_g = swap(maps)

    z2, y1, y1_g, y2, ws4, ws4_g, maps_g = tie(z2, y1, y1_g, y2, ws4, ws4_g, maps_g)
    z3 = spread(z2, "z")
    ends = [slice(DL, 2 * DL), slice(2 * DL, 2 * DL + 4 * PART), slice(2 * DL + 4 * PART, None)]
    yz = spread(
        pack(
            (48, 2 * DL + 8 * PART),
            [(y1, top, (every, left)), (y2, top, (every, ends[0]))]
            + [(ws4, None, (every, ends[1])), (ws4_g, None, (every, ends[2]))],
        ),
        "y",
    )
    y2_g = swap(y2)

    z3, y2_g = tie(z3, y2_g)
    z4 = spread(z3, "z")
    s_got = swap(
        pack(
            (96, KS),
            [
                (s1, slice(32, 64), slice(0, 32)),
                (z2, (slice(32, 64), right), slice(32, 64)),
                (z3, (slice(32, 64), right), slice(64, 96)),
            ],
        )
    )

    z4, yz, s_got = tie(z4, yz, s_got)
    far_s = spread(pack((48, 4 * PART), [(yz, (every, ends[1]), every)]), "y")
    yz_g = swap(yz)
    own, another = call(
        project_body,
        [((384, 256), BF), ((288, 256), BF)],
        (where, a0, z1, z2, z3, z4, w0, y1, y1_g, yz, pr, y2, y2_g),
        limit=12,
        flops=2**32,
    )
    kept, sent = call(
        finish_body,
        [((256, 384), BF)] * 2,
        (where, a0, z1, z2, z3, z4, yz_g, own, another, order_l),
        limit=12,
        flops=2**29,
    )

    taken = flip(sent, "x", 1)
    kept_g = swap(kept)
    far_s, _ = tie(far_s, sent)
    far_s_g = swap(far_s)
    query_s, own_s = call(
        project_small_body,
        [((128, HD), BF), ((128, 2 * HD), BF)],
        (where, s0, s1, z1, z2, z3, s_got, ws4, ws4_g, yz, yz_g, far_s, far_s_g, order_s),
        [pltpu.VMEM((128, DS), BF)],
        limit=6,
        flops=2**29,
    )
    got_s = swap(own_s)
    taken, got_s = tie(taken, got_s)
    x1 = spread(jnp.concatenate([own_s, got_s], 0), "x")
    x2 = flip(own_s, "x", 2)

    pairs = slice(HD, None)
    taken_g = swap(taken)
    all_l = pack(
        (1024, 2 * HD),
        [
            (value, (every, pairs), slice(256 * i, 256 * i + 256))
            for i, value in enumerate((kept, taken, kept_g, taken_g))
        ],
    )
    k_side = spread(all_l, "y")

    x1_g, x2_g = swap(x1), swap(x2)
    first, second = slice(0, 128), slice(128, 256)
    parts = ((own_s, None), (x1, first), (x1_g, second), (x2, None))
    parts += ((got_s, None), (x1, second), (x1_g, first), (x2_g, None))
    all_s = pack(
        (1024, 2 * HD),
        [(value, part, slice(128 * i, 128 * i + 128)) for i, (value, part) in enumerate(parts)],
    )
    s_side = spread(all_s, "y")
    k_side, _ = tie(k_side, all_s)
    k_far = spread(k_side[:512], "y")
    k_side_g = swap(k_side)
    k_far, _ = tie(k_far, s_side)
    k_far_g = swap(k_far)
    s_far = spread(s_side[:512], "y")
    s_side_g = swap(s_side)

    keep, send = call(
        large_body,
        [((32, 8, 128), F32)] * 2,
        (where, kept, taken, maps, maps_g, all_l, k_side, k_side_g, k_far, k_far_g),
        [pltpu.VMEM((256, 4096), F32)] * 2,
        flops=2**32,
    )
    keep, send, s_far = tie(keep, send, s_far)
    got = swap(send)
    s_far_g = swap(s_far)
    (total,) = call(
        small_body,
        [((32, 8, 128), F32)],
        (where, query_s, maps, maps_g, keep, all_s, s_side, s_side_g, s_far, s_far_g),
        [pltpu.VMEM((128, 4096), F32)],
        flops=2**30,
    )

    returned = lax.all_to_all(total + got, ("z", "x"), split_axis=0, concat_axis=0, tiled=True)
    returned = jnp.sum(returned, axis=0)
    latent_l = lax.dynamic_slice_in_dim(latent_large, core * 16, 16, 0)
    latent_s = lax.dynamic_slice_in_dim(latent_small, core * 16, 16, 0)
    direct = GUIDANCE * jnp.dot(latent_l, head_large, preferred_element_type=F32) + (
        1.0 - GUIDANCE
    ) * jnp.dot(latent_s, head_small, preferred_element_type=F32)
    part = direct + jnp.concatenate([returned[:, :64], returned[:, 64:]], 0)
    other_part = swap(part)
    return jnp.where(
        core == 0,
        jnp.concatenate([part, other_part], 0),
        jnp.concatenate([other_part, part], 0),
    )


def solution(mesh):
    grid = Mesh(mesh.devices.reshape(2, 8, 4, 4), ("grp", "z", "x", "y"))
    tokens = ("z", "x", "y")
    return jax.shard_map(
        shards,
        mesh=grid,
        in_specs=(
            P(tokens, None),
            P(tokens, None),
            P(),
            P(),
            P(None, ("grp",) + tokens),
            P(None, ("grp",) + tokens),
            P("grp", None),
            P("grp", None),
            P(),
            P(),
        ),
        out_specs=P(tokens, None),
        check_vma=False,
    )
```
